128 devices in a mesh: dp: 32 (over z, y_hi, x), section: 4 (over y_lo, core).
Axes of the slice: x: 4, y: 4 (y_hi: 2, y_lo: 2; y = y_hi * 2 + y_lo), z: 4, core: 2. Of those that a mesh axis runs over, the one named last changes fastest.
Arguments:
- encoder: bfloat16 [32, 4, 384, 1280], P('dp', 'section'), may hold values from -300 to 300
- destinations: int32 [32, 4, 384, 2], P('dp', 'section'), may hold values from 0 to 31, all different within a row; in each aligned block of 384 rows (0 to 383, 384 to 767, ..., all dimensions but the last counted through in order) at most 48 rows name the same one
- hidden: bfloat16 [32, 4, 256, 1280], P('dp', 'section'), may hold values from -6 to 6
- w_query: bfloat16 [4, 1280, 640], P('section'), may hold values from -0.15625 to 0.15625
- w_key: bfloat16 [4, 1280, 640], P('section'), may hold values from -0.15625 to 0.15625
- w_value: bfloat16 [4, 1280, 640], P('section'), may hold values from -0.15625 to 0.15625
- cotangent: bfloat16 [32, 4, 256, 640], P('dp', 'section'), may hold values from -6 to 6
Outputs:
- attended: bfloat16 [32, 4, 256, 640], P('dp', 'section')
- d_hidden: bfloat16 [32, 4, 256, 1280], P('dp', 'section')
- d_encoder: bfloat16 [32, 4, 384, 1280], P('dp', 'section')
- weight_grads: float32 [4, 1280, 1920], P('section', 'dp')
The draws below stay inside these ranges and needn't reach their ends.
Inputs may be any that keep to these rules, and one draw needn't show every extreme that they name: `destinations`: each frame names two different readers; in the frames of one device at most 48 name the same reader, and that many do in some device.
All inputs are finite; a program needn't handle non-finite values.
Results may differ from the reference program's by a relative error of at most 0.024.
The reference program's roundings to bfloat16 on the way count: a program that leaves them out, or rounds other values in their place, can miss the bound.
Values may be sent and summed in bfloat16 or wider, within the bound.
No kernel may reach another device: no remote copies, remote signals or barrier semaphores. Data moves between devices by JAX's collectives and lax.ppermute only.
A program may use at most 192 MiB of HBM per device.

```python
import math
import jax
import jax.numpy as jnp
import numpy as np
from jax import lax

D = 1280
HEADS = 10
HEAD_DIM = 64
ROWS_DEV = 384
DEC_DEV = 256
HW = 640
CAP = 48
N_DP = 32
N_SECTION = 4


def draw_encoder(key, part):
    first = jax.random.fold_in(key, 0)
    shape = (N_DP, N_SECTION, ROWS_DEV, D)
    values = jnp.clip(jax.random.normal(first, shape, jnp.float32), -6.0, 6.0)
    return values.astype(jnp.bfloat16)


def level_of(own_key, extent, cuts, least, top_value):
    level = 1.0
    for axis_at, parts in cuts:
        draws = jax.random.uniform(jax.random.fold_in(jax.random.fold_in(own_key, 6), axis_at), (parts,), jnp.float32, least / len(cuts), top_value / len(cuts))
        level = level * jnp.repeat(jnp.exp(draws), extent[axis_at] // parts).reshape((-1,) + (1,) * (len(extent) - 1 - axis_at))
    return level


def assign_block(own_key, own, number, rows, count, top, most, slope):
    sequence = jax.random.permutation(own_key, count)
    heavy_load, ordinary = shares(count, rows * top, most, slope, True), shares(count, rows * top, most, slope, False)
    places = jnp.arange(count)

    def named(tallies, offset_by):
        used = int((tallies > 0).sum())
        fixed = max(1, used // 4)
        shifted = fixed + (places - fixed + offset_by * (used - fixed)) % max(1, count - fixed)
        return jnp.zeros((count,), jnp.int32).at[sequence[jnp.where(places < fixed, places, shifted)]].set(jnp.asarray(tallies, jnp.int32))

    tallies = jnp.where(number % 4 == 0, named(heavy_load, number // 4), named(ordinary, number - number // 4 - 1))
    mixed = jax.random.permutation(jax.random.fold_in(own, 3), count)
    giver, sink = mixed[0:count // 2 * 2:2], mixed[1:count // 2 * 2:2]
    room = jnp.minimum(tallies[giver] - 1, most - tallies[sink]) // 2
    room = jnp.where((giver == sequence[0]) | (sink == sequence[0]) | (tallies[sink] == 0), 0, jnp.maximum(room, 0))
    shifted = jax.random.randint(jax.random.fold_in(own, 4), (count // 2,), 0, 1 << 20) % (room + 1)
    tallies = tallies.at[giver].add(-shifted).at[sink].add(shifted)
    items = jnp.searchsorted(jnp.cumsum(tallies), jnp.arange(rows * top), side="right").astype(jnp.int32)
    table = items.reshape(top, rows).T
    table = table[jax.random.permutation(jax.random.fold_in(own, 1), rows)]
    offset_by = jax.random.randint(jax.random.fold_in(own, 2), (rows, 1), 0, top)
    return jnp.take_along_axis(table, (jnp.arange(top)[None, :] + offset_by) % top, axis=1)


def shares(count, total, most, lean, full):
    weights = [(1 << 20) // math.isqrt(standing ** lean) + 1 for standing in range(1, count + 1)]
    largest = most if full else min(most, max(-(-total // count), total * weights[0] // sum(weights)))
    least = 1 if total - largest >= count - 1 else 0
    holding, rest = [largest] + [least] * (count - 1), total - largest - least * (count - 1)
    while rest > 0:
        movable = [i for i in range(1, count) if holding[i] < largest] or [i for i in range(1, count) if holding[i] < most]
        whole, remaining = sum([weights[i] for i in movable]), rest
        for i in movable:
            addition = min(most - holding[i], max(1, remaining * weights[i] // whole), rest)
            holding[i] = holding[i] + addition
            rest = rest - addition
    return np.array(holding)


def scatter_about(rng, dims, width, reach, cuts=(), held_as=jnp.bfloat16):
    values = jax.random.normal(rng, dims, jnp.float32) * width
    if len(cuts) > 0:
        values = level_of(rng, dims, cuts, -0.22, 0.18) * values
    return jnp.clip(values, min=-reach, max=reach).astype(held_as)


def setup_inputs(seed: int = 0) -> dict:
    arg_keys = jax.random.split(jax.random.key(seed), 8)
    encoder = draw_encoder(jax.random.fold_in(arg_keys[7], 71), 0)
    destinations_keys = jax.random.split(jax.random.fold_in(arg_keys[1], 1), N_DP * N_SECTION * ROWS_DEV // ROWS_DEV)
    destinations_turns = jax.random.permutation(jax.random.fold_in(arg_keys[1], 3), N_DP * N_SECTION * ROWS_DEV // ROWS_DEV)
    destinations = jax.vmap(lambda own, number: assign_block(jax.random.fold_in(arg_keys[1], 2), own, number, ROWS_DEV, N_DP, 2, CAP, 2))(destinations_keys, destinations_turns).reshape((N_DP, N_SECTION, ROWS_DEV, 2))
    hidden = scatter_about(arg_keys[2], (N_DP, N_SECTION, DEC_DEV, D), 1.0, 6.0, ((0, 32), (1, 4)))
    w_query = scatter_about(arg_keys[3], (N_SECTION, D, HW), D ** -0.5, 0.15625, ((0, 4),))
    w_key = scatter_about(arg_keys[4], (N_SECTION, D, HW), D ** -0.5, 0.15625, ((0, 4),))
    w_value = scatter_about(arg_keys[5], (N_SECTION, D, HW), D ** -0.5, 0.15625, ((0, 4),))
    cotangent = scatter_about(arg_keys[6], (N_DP, N_SECTION, DEC_DEV, HW), 1.0, 6.0, ((0, 32), (1, 4)))
    return dict(encoder=encoder, destinations=destinations, hidden=hidden, w_query=w_query, w_key=w_key, w_value=w_value, cotangent=cotangent)


SCALE = 0.125


def placement_table(dest_col, reader):
    hit = jnp.any(dest_col == reader, axis=-1)
    position = jnp.cumsum(hit.astype(jnp.int32), axis=1) - 1
    slots = jnp.arange(CAP, dtype=jnp.int32)
    table = jnp.logical_and(hit[:, None, :], position[:, None, :] == slots[None, :, None])
    return table.astype(jnp.float32)


def attend(queries, keys, values, valid, cot):
    dec = queries.shape[0]
    total = keys.shape[0]
    q_heads = queries.astype(jnp.float32).reshape(dec, HEADS, HEAD_DIM)
    k_heads = keys.astype(jnp.float32).reshape(total, HEADS, HEAD_DIM)
    v_heads = values.astype(jnp.float32).reshape(total, HEADS, HEAD_DIM)
    g_heads = cot.astype(jnp.float32).reshape(dec, HEADS, HEAD_DIM)
    scores = jnp.einsum('ihd,jhd->hij', q_heads, k_heads) * SCALE
    scores = jnp.where(valid[None, None, :] > 0, scores, -1e30)
    top = jnp.max(scores, axis=-1, keepdims=True)
    expo = jnp.exp(scores - top)
    probs = expo / jnp.sum(expo, axis=-1, keepdims=True)
    probs_b = probs.astype(jnp.bfloat16).astype(jnp.float32)
    output = jnp.einsum('hij,jhd->ihd', probs_b, v_heads).reshape(dec, HW).astype(jnp.bfloat16)
    dprobs = jnp.einsum('ihd,jhd->hij', g_heads, v_heads)
    dscores = probs * (dprobs - jnp.sum(probs * dprobs, axis=-1, keepdims=True))
    dscores = dscores.astype(jnp.bfloat16).astype(jnp.float32)
    dq = (jnp.einsum('hij,jhd->ihd', dscores, k_heads) * SCALE).reshape(dec, HW).astype(jnp.bfloat16)
    dk = (jnp.einsum('hij,ihd->jhd', dscores, q_heads) * SCALE).reshape(total, HW).astype(jnp.bfloat16)
    dv = jnp.einsum('hij,ihd->jhd', probs_b, g_heads).reshape(total, HW).astype(jnp.bfloat16)
    return output, dq, dk, dv


def reference(encoder, destinations, hidden, w_query, w_key, w_value, cotangent):
    attended_cols = []
    encoder_cols = []
    grads_cols = []
    dhidden_cols = [None] * N_SECTION
    for section in range(N_SECTION):
        enc_col = encoder[:, section]
        enc_float = enc_col.astype(jnp.float32)
        dest_col = destinations[:, section]
        wq = w_query[section]
        wk = w_key[section]
        wv = w_value[section]
        before = (section - 1) % N_SECTION
        hid_col = hidden[:, before]
        cot_col = cotangent[:, section]

        def visit(carry, reader):
            totals, grads = carry
            table = placement_table(dest_col, reader)
            received = jnp.einsum('acr,ard->acd', table, enc_float).astype(jnp.bfloat16).reshape(-1, D)
            own = lax.dynamic_index_in_dim(enc_col, reader, 0, keepdims=False)
            memory = jnp.concatenate([own, received], axis=0)
            valid = jnp.concatenate([jnp.ones((ROWS_DEV,), jnp.float32), jnp.sum(table, axis=-1).reshape(-1)])
            entering = lax.dynamic_index_in_dim(hid_col, reader, 0, keepdims=False)
            cot = lax.dynamic_index_in_dim(cot_col, reader, 0, keepdims=False)
            queries = jnp.dot(entering, wq, preferred_element_type=jnp.float32).astype(jnp.bfloat16)
            keys = jnp.dot(memory, wk, preferred_element_type=jnp.float32).astype(jnp.bfloat16)
            values = jnp.dot(memory, wv, preferred_element_type=jnp.float32).astype(jnp.bfloat16)
            output, dq, dk, dv = attend(queries, keys, values, valid, cot)
            grad_q = jnp.dot(entering.T, dq, preferred_element_type=jnp.float32)
            grad_k = jnp.dot(memory.T, dk, preferred_element_type=jnp.float32)
            grad_v = jnp.dot(memory.T, dv, preferred_element_type=jnp.float32)
            grads = grads + jnp.concatenate([grad_q, grad_k, grad_v], axis=1)
            dentering = jnp.dot(dq, wq.T, preferred_element_type=jnp.float32).astype(jnp.bfloat16)
            dkv = jnp.concatenate([dk, dv], axis=1).astype(jnp.float32)
            returned = dkv[ROWS_DEV:].reshape(N_DP, CAP, 2 * HW)
            totals = totals + jnp.einsum('acr,ace->are', table, returned)
            totals = totals.at[reader].add(dkv[:ROWS_DEV])
            return (totals, grads), (output, dentering)

        start = (jnp.zeros((N_DP, ROWS_DEV, 2 * HW), jnp.float32), jnp.zeros((D, 3 * HW), jnp.float32))
        (totals, grads), (outputs, dentering) = lax.scan(visit, start, jnp.arange(N_DP, dtype=jnp.int32))
        d_enc = jnp.einsum('are,de->ard', totals[..., :HW], wk.astype(jnp.float32), precision=lax.Precision.HIGHEST)
        d_enc = d_enc + jnp.einsum('are,de->ard', totals[..., HW:], wv.astype(jnp.float32), precision=lax.Precision.HIGHEST)
        attended_cols.append(outputs)
        encoder_cols.append(d_enc.astype(jnp.bfloat16))
        grads_cols.append(grads)
        dhidden_cols[before] = dentering
    attended = jnp.stack(attended_cols, axis=1)
    d_hidden = jnp.stack(dhidden_cols, axis=1)
    d_encoder = jnp.stack(encoder_cols, axis=1)
    weight_grads = jnp.stack(grads_cols, axis=0)
    return attended, d_hidden, d_encoder, weight_grads
```

```python
import jax
import jax.numpy as jnp
from jax import lax
from jax.sharding import PartitionSpec as P

HEADS = 10
HEAD_DIM = 64


SCALE = 0.125


def passed_along(value, axis, steps):
    count = lax.axis_size(axis)
    pairs = [(source, (source + steps) % count) for source in range(count)]
    return lax.ppermute(value, axis, pairs)


def attend(queries, keys, values, valid, cot):
    dec = queries.shape[0]
    total = keys.shape[0]
    q_heads = queries.reshape(dec, HEADS, HEAD_DIM)
    k_heads = keys.reshape(total, HEADS, HEAD_DIM)
    v_heads = values.reshape(total, HEADS, HEAD_DIM)
    g_heads = cot.reshape(dec, HEADS, HEAD_DIM)
    scores = (
        jnp.einsum("ihd,jhd->hij", q_heads, k_heads, preferred_element_type=jnp.float32) * SCALE
    )
    scores = jnp.where(valid[None, None, :] > 0, scores, -1e30)
    top = jnp.max(scores, axis=-1, keepdims=True)
    expo = jnp.exp(scores - top)
    probs = expo / jnp.sum(expo, axis=-1, keepdims=True)
    probs_b = probs.astype(jnp.bfloat16)
    output = jnp.einsum("hij,jhd->ihd", probs_b, v_heads, preferred_element_type=jnp.float32)
    output = output.reshape(dec, HEADS * HEAD_DIM).astype(jnp.bfloat16)
    dprobs = jnp.einsum("ihd,jhd->hij", g_heads, v_heads, preferred_element_type=jnp.float32)
    dscores = (probs * (dprobs - jnp.sum(probs * dprobs, axis=-1, keepdims=True))).astype(
        jnp.bfloat16
    )
    dq = jnp.einsum("hij,jhd->ihd", dscores, k_heads, preferred_element_type=jnp.float32) * SCALE
    dk = jnp.einsum("hij,ihd->jhd", dscores, q_heads, preferred_element_type=jnp.float32) * SCALE
    dv = jnp.einsum("hij,ihd->jhd", probs_b, g_heads, preferred_element_type=jnp.float32)
    dq = dq.reshape(dec, HEADS * HEAD_DIM).astype(jnp.bfloat16)
    dk = dk.reshape(total, HEADS * HEAD_DIM).astype(jnp.bfloat16)
    dv = dv.reshape(total, HEADS * HEAD_DIM).astype(jnp.bfloat16)
    return (output, dq, dk, dv)


def split_parts(values):
    upper = values.astype(jnp.bfloat16)
    lower = (values - upper.astype(jnp.float32)).astype(jnp.bfloat16)
    return (upper, lower)


def per_device(encoder, destinations, hidden, w_query, w_key, w_value, cotangent):
    own = encoder[0, 0]
    dest = destinations[0, 0]
    wq = w_query[0]
    wk = w_key[0]
    wv = w_value[0]
    rows = own.shape[0]
    width = own.shape[1]
    heads_width = wq.shape[1]
    readers = lax.axis_size("dp")
    capacity = 4 * rows // readers
    targets = jnp.arange(readers, dtype=jnp.int32)
    hit = jnp.any(dest[None, :, :] == targets[:, None, None], axis=-1)
    order = jnp.arange(rows, dtype=jnp.int32)
    upto = (order[:, None] <= order[None, :]).astype(jnp.bfloat16)
    position = jnp.dot(hit.astype(jnp.bfloat16), upto, preferred_element_type=jnp.float32)
    position = position.astype(jnp.int32) - 1
    slots = jnp.arange(capacity, dtype=jnp.int32)
    table = jnp.logical_and(hit[:, None, :], position[:, None, :] == slots[None, :, None])
    table = table.astype(jnp.bfloat16)
    filled = jnp.sum(table.astype(jnp.float32), axis=-1).astype(jnp.bfloat16)
    w_both = jnp.concatenate([wk, wv], axis=1)
    entering = passed_along(hidden[0, 0], "section", 1)
    queries = jnp.dot(entering, wq, preferred_element_type=jnp.float32).astype(jnp.bfloat16)
    outgoing = jnp.einsum("bcr,rd->bcd", table, own, preferred_element_type=jnp.float32).astype(
        jnp.bfloat16
    )
    arrived, flags = (
        lax.all_to_all(outgoing, "dp", split_axis=0, concat_axis=0, tiled=True),
        lax.all_to_all(filled, "dp", split_axis=0, concat_axis=0, tiled=True),
    )
    memory = jnp.concatenate([own, arrived.reshape(-1, width)], axis=0)
    kv_all = jnp.dot(memory, w_both, preferred_element_type=jnp.float32).astype(jnp.bfloat16)
    keys = kv_all[:, :heads_width]
    values = kv_all[:, heads_width:]
    valid = jnp.concatenate([jnp.ones((rows,), jnp.float32), flags.reshape(-1).astype(jnp.float32)])
    output, dq, dk, dv = attend(queries, keys, values, valid, cotangent[0, 0])
    dentering = jnp.dot(dq, wq.T, preferred_element_type=jnp.float32).astype(jnp.bfloat16)
    d_hidden = passed_along(dentering, "section", -1)
    dkv = jnp.concatenate([dk, dv], axis=1)
    slot_grads = dkv[rows:].reshape(readers, capacity, 2 * heads_width)
    returned = lax.all_to_all(slot_grads, "dp", split_axis=0, concat_axis=0, tiled=True)
    totals = dkv[:rows].astype(jnp.float32)
    totals = totals + jnp.einsum("bcr,bce->re", table, returned, preferred_element_type=jnp.float32)
    upper, lower = split_parts(totals)
    back = (((1,), (1,)), ((), ()))
    d_enc = lax.dot_general(upper, w_both, back, preferred_element_type=jnp.float32)
    d_enc = d_enc + lax.dot_general(lower, w_both, back, preferred_element_type=jnp.float32)
    d_enc = d_enc.astype(jnp.bfloat16)
    contract = (((0,), (0,)), ((), ()))
    part_q = lax.dot_general(entering, dq, contract, preferred_element_type=jnp.float32)
    part_kv = lax.dot_general(memory, dkv, contract, preferred_element_type=jnp.float32)
    grads = lax.psum_scatter(
        jnp.concatenate([part_q, part_kv], axis=1), "dp", scatter_dimension=0, tiled=True
    )
    return (output[None, None], d_hidden[None, None], d_enc[None, None], grads[None])


def solution(mesh):
    return jax.shard_map(
        per_device,
        mesh=mesh,
        in_specs=(
            P("dp", "section", None, None),
            P("dp", "section", None, None),
            P("dp", "section", None, None),
            P("section", None, None),
            P("section", None, None),
            P("section", None, None),
            P("dp", "section", None, None),
        ),
        out_specs=(
            P("dp", "section", None, None),
            P("dp", "section", None, None),
            P("dp", "section", None, None),
            P("section", "dp", None),
        ),
        check_vma=False,
    )
```

```python
import functools

import jax
import jax.numpy as jnp
from jax import lax
from jax.experimental import pallas as pl
from jax.experimental.pallas import tpu as pltpu
from jax.sharding import PartitionSpec as P

PAIR = 128
CHUNKS = (2, 3)
SLOTS, ROWS, TWICE = 48, 40, 24
SENT = SLOTS + ROWS + TWICE
SCALE = 0.125
F32 = jnp.float32
BF16 = jnp.bfloat16
VMEM_LIMIT = 60 * 1024 * 1024

NT = (((1,), (1,)), ((), ()))
NN = (((1,), (0,)), ((), ()))


def mm(a, b, dims=NN):
    return lax.dot_general(a, b, dims, preferred_element_type=F32)


def params(**kw):
    return pltpu.CompilerParams(vmem_limit_bytes=VMEM_LIMIT, **kw)


def cost(flops, bytes_accessed, transcendentals=0):
    return pl.CostEstimate(
        flops=flops, bytes_accessed=bytes_accessed, transcendentals=transcendentals
    )


def passed_along(value, axis, steps):
    count = lax.axis_size(axis)
    pairs = [(source, (source + steps) % count) for source in range(count)]
    return lax.ppermute(value, axis, pairs)


def exchanged(value):
    return lax.all_to_all(value, "dp", split_axis=0, concat_axis=0, tiled=True)


def slots_along_lanes(dc, dr, capacity):
    rows = dr.shape[1]
    shape = (rows, rows)
    before = lax.broadcasted_iota(jnp.int32, shape, 0) < lax.broadcasted_iota(
        jnp.int32, shape, 1
    )
    found = []
    for which in range(2):
        mine = dr[which : which + 1, :]
        same = jnp.logical_or(dc[:, 0:1] == mine, dc[:, 1:2] == mine)
        earlier = jnp.where(jnp.logical_and(same, before), 1.0, 0.0)
        place = jnp.sum(earlier, axis=0, keepdims=True).astype(jnp.int32)
        found.append(mine * capacity + place)
    return found


def slots_along_sublanes(dc, dr, capacity):
    rows = dr.shape[1]
    shape = (rows, rows)
    before = lax.broadcasted_iota(jnp.int32, shape, 1) < lax.broadcasted_iota(
        jnp.int32, shape, 0
    )
    found = []
    for which in range(2):
        mine = dc[:, which : which + 1]
        same = jnp.logical_or(dr[0:1, :] == mine, dr[1:2, :] == mine)
        earlier = jnp.where(jnp.logical_and(same, before), 1.0, 0.0)
        place = jnp.sum(earlier, axis=1, keepdims=True).astype(jnp.int32)
        found.append(mine * capacity + place)
    return found


def dispatch_kernel(capacity, dc_ref, dr_ref, own_ref, out_ref):
    rows = own_ref.shape[0]
    both = jnp.concatenate([own_ref[...], jnp.ones((rows, PAIR), BF16)], axis=1)
    slot_a, slot_b = slots_along_lanes(dc_ref[...], dr_ref[...], capacity)
    for block in range(out_ref.shape[0] // rows):
        at = lax.broadcasted_iota(jnp.int32, (rows, rows), 0) + block * rows
        table = jnp.logical_or(at == slot_a, at == slot_b)
        table = jnp.where(table, 1.0, 0.0).astype(BF16)
        out_ref[pl.ds(block * rows, rows), :] = mm(table, both).astype(BF16)


def dispatch(capacity, readers, dc, dr, own):
    rows, width = own.shape
    slots = readers * capacity
    return pl.pallas_call(
        functools.partial(dispatch_kernel, capacity),
        out_shape=jax.ShapeDtypeStruct((slots, width + PAIR), BF16),
        compiler_params=params(),
        cost_estimate=cost(2 * rows * width * slots, 2 * width * (rows + slots)),
        name="dispatch",
    )(dc, dr, own)


def attend_kernel(held, *refs):
    q_ref, g_ref, own_ref, got_ref, wk_ref, wv_ref, entering_ref = refs[:7]
    o_ref, dq_ref, down_ref, sent_ref = refs[7 + held : 11 + held]
    kv_ref, s_ref, dp_ref, mem_t_ref, entering_t_ref = refs[11 + held :]
    readers = sent_ref.shape[0]
    dec = q_ref.shape[0]
    tile, width = own_ref.shape
    tiles = 1 + got_ref.shape[0] // tile
    lane = lax.broadcasted_iota(jnp.int32, (dec, PAIR), 1)
    q = q_ref[...] * jnp.asarray(SCALE, BF16)
    g = g_ref[...]
    zero = jnp.zeros_like(q)
    head = [lane < PAIR // 2, lane >= PAIR // 2]
    q_both = jnp.concatenate([jnp.where(head[h], q, zero) for h in range(2)], axis=0)
    g_both = jnp.concatenate([jnp.where(head[h], g, zero) for h in range(2)], axis=0)
    weights = jnp.concatenate([wk_ref[...], wv_ref[...]], axis=1)

    def frames(t):
        if t == 0:
            return own_ref[...]
        return got_ref[pl.ds((t - 1) * tile, tile), :width]

    @pl.when(pl.program_id(0) == 0)
    def _():
        for t in range(tiles):
            mem_t_ref[:, t * tile : (t + 1) * tile] = frames(t).T
        entering_t_ref[...] = entering_ref[...].T

    tops = []
    for t in range(tiles):
        at = pl.ds(t * tile, tile)
        kv = mm(frames(t), weights).astype(BF16)
        kv_ref[at, :] = kv
        s = mm(kv[:, :PAIR], q_both, NT)
        if t > 0:
            flag = got_ref[pl.ds((t - 1) * tile, tile), width : width + PAIR]
            s = s + (flag.astype(F32)[:, 0:1] - 1.0) * 1e30
        s_ref[at, :] = s
        tops.append(jnp.max(s, axis=0, keepdims=True))
    top = functools.reduce(jnp.maximum, tops)
    total = jnp.zeros_like(top)
    inner = jnp.zeros_like(top)
    for t in range(tiles):
        at = pl.ds(t * tile, tile)
        e = jnp.exp(s_ref[at, :] - top)
        s_ref[at, :] = e
        total = total + jnp.sum(e, axis=0, keepdims=True)
        dp = mm(kv_ref[at, PAIR:], g_both, NT)
        dp_ref[at, :] = dp
        inner = inner + jnp.sum(e * dp, axis=0, keepdims=True)
    inverse = 1.0 / total
    inner = inner * inverse
    half = PAIR // 2
    out_t = [jnp.zeros((half, dec), F32) for _ in range(2)]
    dq_t = [jnp.zeros((half, dec), F32) for _ in range(2)]
    for t in range(tiles):
        at = pl.ds(t * tile, tile)
        kv_t = kv_ref[at, :].T
        p = s_ref[at, :] * inverse
        pb = p.astype(BF16)
        ds = (p * (dp_ref[at, :] - inner)).astype(BF16)
        for h in range(2):
            cols = slice(h * dec, (h + 1) * dec)
            dq_t[h] = dq_t[h] + mm(kv_t[h * half : (h + 1) * half], ds[:, cols])
            out_t[h] = out_t[h] + mm(kv_t[PAIR + h * half : PAIR + (h + 1) * half], pb[:, cols])
        dk = mm(ds, q_both)
        dv = mm(pb, g_both)
        dkv = jnp.concatenate([dk, dv], axis=1).astype(BF16)
        kv_ref[at, :] = dkv
        if t == 0:
            down_ref[...] = dkv
        else:
            count = tile // SLOTS
            dkv = dkv.reshape(count, SLOTS, 2 * PAIR)
            sent_ref[pl.ds((t - 1) * count, count), :SLOTS, :] = dkv
    o_ref[...] = jnp.concatenate(out_t, axis=0).T.astype(BF16)
    dq = (jnp.concatenate(dq_t, axis=0) * SCALE).T.astype(BF16)
    dq_ref[...] = dq
    grad = mm(mem_t_ref[...], kv_ref[...]).reshape(readers, ROWS, 2 * PAIR)
    sent_ref[:, SLOTS : SLOTS + ROWS, :] = grad.astype(BF16)
    grad = mm(entering_t_ref[...], dq).reshape(readers, ROWS, PAIR)
    grad = jnp.concatenate([grad[:, :TWICE], grad[:, ROWS - TWICE :]], axis=2)
    sent_ref[:, SLOTS + ROWS :, :] = grad.astype(BF16)


def attend(first, pairs, readers, queries, cot, own, got, wk, wv, entering, filled):
    dec, heads = queries.shape
    rows, width = own.shape
    slots = got.shape[0]
    total = rows + slots
    pair_at = lambda p: (0, first + p)
    whole = lambda p: (0, 0)
    return pl.pallas_call(
        functools.partial(attend_kernel, len(filled)),
        grid=(pairs,),
        in_specs=[
            pl.BlockSpec((dec, PAIR), pair_at),
            pl.BlockSpec((dec, PAIR), pair_at),
            pl.BlockSpec((rows, width), whole),
            pl.BlockSpec((slots, width + PAIR), whole),
            pl.BlockSpec((width, PAIR), pair_at),
            pl.BlockSpec((width, PAIR), pair_at),
            pl.BlockSpec((dec, width), whole),
        ]
        + [pl.BlockSpec(memory_space=pl.ANY)] * len(filled),
        out_specs=[
            pl.BlockSpec((dec, PAIR), pair_at),
            pl.BlockSpec((dec, PAIR), pair_at),
            pl.BlockSpec((rows, 2 * PAIR), pair_at),
            pl.BlockSpec((readers, SENT, 2 * PAIR), lambda p: (0, 0, p)),
        ],
        out_shape=(
            jax.ShapeDtypeStruct((dec, heads), BF16),
            jax.ShapeDtypeStruct((dec, heads), BF16),
            jax.ShapeDtypeStruct((rows, 2 * heads), BF16),
            jax.ShapeDtypeStruct((readers, SENT, 2 * PAIR * pairs), BF16),
        ),
        scratch_shapes=[
            pltpu.VMEM((total, 2 * PAIR), BF16),
            pltpu.VMEM((total, 2 * dec), F32),
            pltpu.VMEM((total, 2 * dec), F32),
            pltpu.VMEM((width, total), BF16),
            pltpu.VMEM((width, dec), BF16),
        ],
        input_output_aliases={7 + i: i for i in range(len(filled))},
        compiler_params=params(dimension_semantics=("arbitrary",)),
        cost_estimate=cost(
            pairs * (12 * dec * total * PAIR * 4 + 8 * width * total * PAIR),
            2 * total * width + pairs * 12 * total * PAIR,
            pairs * 2 * dec * total,
        ),
        name=f"attend_{first}",
    )(queries, cot, own, got, wk, wv, entering, *filled)


def query_kernel(dq_ref, wq_ref, dent_ref):
    dent_ref[...] = mm(dq_ref[...], wq_ref[...], NT).astype(BF16)


def query_side(dq, wq):
    dec = dq.shape[0]
    width, heads = wq.shape
    return pl.pallas_call(
        query_kernel,
        out_shape=jax.ShapeDtypeStruct((dec, width), BF16),
        compiler_params=params(),
        cost_estimate=cost(2 * dec * width * heads, 2 * width * (dec + heads)),
        name="query_side",
    )(dq, wq)


def combine_kernel(first, capacity, last, dc_ref, dr_ref, down_ref, back_ref, wk_ref, wv_ref, *refs):
    held, out_ref = refs[:-1], refs[-1]
    rows = down_ref.shape[0]
    lanes = back_ref.shape[2]
    slot_a, slot_b = slots_along_sublanes(dc_ref[...], dr_ref[...], capacity)
    tot = down_ref[:, 2 * first * PAIR : 2 * first * PAIR + lanes].astype(F32)
    count = rows // SLOTS
    for block in range(back_ref.shape[0] // count):
        at = lax.broadcasted_iota(jnp.int32, (rows, rows), 1) + block * rows
        table = jnp.logical_or(at == slot_a, at == slot_b)
        table = jnp.where(table, 1.0, 0.0).astype(BF16)
        part = back_ref[pl.ds(block * count, count), :, :].reshape(rows, lanes)
        tot = tot + mm(table, part)
    tot = tot.astype(BF16)
    pieces = [tot[:, c * PAIR : (c + 1) * PAIR] for c in range(lanes // PAIR)]
    cut = slice(first * PAIR, first * PAIR + lanes // 2)
    out = mm(jnp.concatenate(pieces[0::2], axis=1), wk_ref[:, cut], NT)
    out = out + mm(jnp.concatenate(pieces[1::2], axis=1), wv_ref[:, cut], NT)
    for r in held:
        out = out + r[...]
    out_ref[...] = out.astype(out_ref.dtype)


def combine(first, last, capacity, dc, dr, down, back, wk, wv, held):
    rows = down.shape[0]
    width, heads = wk.shape
    readers, _, lanes = back.shape
    whole = lambda i: (0, 0)
    full = lambda a: pl.BlockSpec(a.shape, whole)
    return pl.pallas_call(
        functools.partial(combine_kernel, first, capacity, last),
        grid=(1,),
        in_specs=[
            full(dc),
            full(dr),
            full(down),
            pl.BlockSpec((readers, SLOTS, lanes), lambda i: (0, 0, 0)),
            full(wk),
            full(wv),
        ]
        + [full(h) for h in held],
        out_specs=pl.BlockSpec((rows, width), whole),
        out_shape=jax.ShapeDtypeStruct((rows, width), BF16 if last else F32),
        compiler_params=params(),
        cost_estimate=cost(
            2 * rows * lanes * (width + readers * SLOTS),
            2 * (rows * width + width * lanes + readers * SLOTS * lanes),
        ),
        name=f"combine_{first}",
    )(dc, dr, down, back, wk, wv, *held)


def sum_kernel(back_ref, out_ref):
    sums = [back_ref[a].astype(F32) for a in range(4)]
    for a in range(4, back_ref.shape[0]):
        sums[a % 4] = sums[a % 4] + back_ref[a].astype(F32)
    out_ref[...] = (sums[0] + sums[1]) + (sums[2] + sums[3])


def summed(first, back):
    readers, rows, lanes = back.shape
    step = 16
    return pl.pallas_call(
        sum_kernel,
        grid=((rows - SLOTS) // step,),
        in_specs=[pl.BlockSpec((readers, step, lanes), lambda i: (0, SLOTS // step + i, 0))],
        out_specs=pl.BlockSpec((step, lanes), lambda i: (i, 0)),
        out_shape=jax.ShapeDtypeStruct((rows - SLOTS, lanes), F32),
        compiler_params=params(),
        cost_estimate=cost(readers * rows * lanes, 2 * readers * rows * lanes),
        name=f"summed_{first}",
    )(back)


def gather_kernel(*refs):
    parts, out_ref = refs[:-1], refs[-1]
    heads = out_ref.shape[1] // 3
    both = jnp.concatenate([r[...] for r in parts], axis=1)
    pieces = [both[:, c * PAIR : (c + 1) * PAIR] for c in range(2 * heads // PAIR)]
    upper = jnp.concatenate(pieces[0::2], axis=1)
    lower = jnp.concatenate(pieces[1::2], axis=1)
    out_ref[:TWICE, :heads] = upper[ROWS:]
    out_ref[TWICE:, :heads] = lower[2 * TWICE :]
    out_ref[:, heads : 2 * heads] = upper[:ROWS]
    out_ref[:, 2 * heads :] = lower[:ROWS]


def gathered(heads, parts):
    return pl.pallas_call(
        gather_kernel,
        out_shape=jax.ShapeDtypeStruct((ROWS, 3 * heads), F32),
        compiler_params=params(),
        cost_estimate=cost(0, 24 * ROWS * heads),
        name="gathered",
    )(*parts)


def per_device(encoder, destinations, hidden, w_query, w_key, w_value, cotangent):
    own = encoder[0, 0]
    dest = destinations[0, 0]
    wq, wk, wv = w_query[0], w_key[0], w_value[0]
    cot = cotangent[0, 0]
    rows, width = own.shape
    heads = wq.shape[1]
    readers = lax.axis_size("dp")
    capacity = 4 * rows // readers
    dest_rows = dest.T

    slots = readers * capacity

    slots = readers * capacity

    entering = passed_along(hidden[0, 0], "section", 1)
    out = dispatch(capacity, readers, dest, dest_rows, own)
    out, entering = lax.optimization_barrier((out, entering))
    queries = jnp.dot(entering, wq, preferred_element_type=F32).astype(BF16)
    got = exchanged(out.reshape(readers, capacity, -1)).reshape(slots, -1)

    filled, backs, firsts, first = (), [], [], 0
    for pairs in CHUNKS:
        *filled, sent = attend(
            first, pairs, readers, queries, cot, own, got, wk, wv, entering, filled
        )
        backs.append(exchanged(sent))
        firsts.append(first)
        first += pairs
    attended, dq, down = filled
    dentering = query_side(dq, wq)
    held, grads = [], []
    for c, first in enumerate(firsts):
        last = c == len(firsts) - 1
        if held:
            backs[c], held, grads, down, dentering = lax.optimization_barrier(
                (backs[c], held, grads, down, dentering)
            )
        if last:
            d_hidden = passed_along(dentering, "section", -1)
        held = [
            combine(first, last, capacity, dest, dest_rows, down, backs[c], wk, wv, held)
        ]
        grads.append(summed(first, backs[c]))
    d_enc = held[0]
    grads = gathered(heads, grads)
    return (attended[None, None], d_hidden[None, None], d_enc[None, None], grads[None])


def solution(mesh):
    return jax.shard_map(
        per_device,
        mesh=mesh,
        in_specs=(
            P("dp", "section", None, None),
            P("dp", "section", None, None),
            P("dp", "section", None, None),
            P("section", None, None),
            P("section", None, None),
            P("section", None, None),
            P("dp", "section", None, None),
        ),
        out_specs=(
            P("dp", "section", None, None),
            P("dp", "section", None, None),
            P("dp", "section", None, None),
            P("section", "dp", None),
        ),
        check_vma=False,
    )
```

```python
import functools

import jax
import jax.numpy as jnp
from jax import lax
from jax.experimental import pallas as pl
from jax.experimental.pallas import tpu as pltpu
from jax.sharding import PartitionSpec as P

PAIR = 128
CHUNKS = (2, 3)
ROWS, TWICE, SLOTS = 40, 24, 48
GRADS = ROWS + TWICE
SENT = GRADS + SLOTS
STEP = 16
SCALE = 0.125
F32 = jnp.float32
BF16 = jnp.bfloat16
VMEM_LIMIT = 60 * 1024 * 1024

NT = (((1,), (1,)), ((), ()))
NN = (((1,), (0,)), ((), ()))


def mm(a, b, dims=NN):
    return lax.dot_general(a, b, dims, preferred_element_type=F32)


def params(**kw):
    return pltpu.CompilerParams(vmem_limit_bytes=VMEM_LIMIT, **kw)


def cost(flops, bytes_accessed, transcendentals=0):
    return pl.CostEstimate(
        flops=flops, bytes_accessed=bytes_accessed, transcendentals=transcendentals
    )


def passed_along(value, axis, steps):
    count = lax.axis_size(axis)
    pairs = [(source, (source + steps) % count) for source in range(count)]
    return lax.ppermute(value, axis, pairs)


def exchanged(value):
    return lax.all_to_all(value, "dp", split_axis=0, concat_axis=0, tiled=True)


def down_the_rows(dr):
    filler = jnp.zeros((8 - dr.shape[0], dr.shape[1]), F32)
    return jnp.concatenate([dr.astype(F32), filler], axis=0).T.astype(jnp.int32)


def slots_along_lanes(dr, capacity):
    dc = down_the_rows(dr)
    rows = dr.shape[1]
    shape = (rows, rows)
    before = lax.broadcasted_iota(jnp.int32, shape, 0) < lax.broadcasted_iota(
        jnp.int32, shape, 1
    )
    found = []
    for which in range(2):
        mine = dr[which : which + 1, :]
        same = jnp.logical_or(dc[:, 0:1] == mine, dc[:, 1:2] == mine)
        earlier = jnp.where(jnp.logical_and(same, before), 1.0, 0.0)
        place = jnp.sum(earlier, axis=0, keepdims=True).astype(jnp.int32)
        found.append(mine * capacity + place)
    return found


def slots_along_sublanes(dr, capacity):
    dc = down_the_rows(dr)
    rows = dr.shape[1]
    shape = (rows, rows)
    before = lax.broadcasted_iota(jnp.int32, shape, 1) < lax.broadcasted_iota(
        jnp.int32, shape, 0
    )
    found = []
    for which in range(2):
        mine = dc[:, which : which + 1]
        same = jnp.logical_or(dr[0:1, :] == mine, dr[1:2, :] == mine)
        earlier = jnp.where(jnp.logical_and(same, before), 1.0, 0.0)
        place = jnp.sum(earlier, axis=1, keepdims=True).astype(jnp.int32)
        found.append(mine * capacity + place)
    return found


def dispatch_kernel(capacity, dr_ref, own_ref, out_ref, slot_ref):
    rows = own_ref.shape[0]
    block = pl.program_id(0)

    @pl.when(block == 0)
    def _():
        for which, slot in enumerate(slots_along_lanes(dr_ref[...], capacity)):
            slot_ref[which : which + 1, :] = slot

    at = lax.broadcasted_iota(jnp.int32, (rows, rows), 0) + block * rows
    table = jnp.logical_or(at == slot_ref[0:1, :], at == slot_ref[1:2, :])
    table = jnp.where(table, 1.0, 0.0).astype(BF16)
    both = jnp.concatenate([own_ref[...], jnp.ones((rows, PAIR), BF16)], axis=1)
    out_ref[...] = mm(table, both).astype(BF16)


def dispatch(capacity, readers, dr, own):
    rows, width = own.shape
    slots = readers * capacity
    whole = lambda i: (0, 0)
    return pl.pallas_call(
        functools.partial(dispatch_kernel, capacity),
        grid=(slots // rows,),
        in_specs=[pl.BlockSpec(dr.shape, whole), pl.BlockSpec((rows, width), whole)],
        out_specs=pl.BlockSpec((rows, width + PAIR), lambda i: (i, 0)),
        out_shape=jax.ShapeDtypeStruct((slots, width + PAIR), BF16),
        scratch_shapes=[pltpu.VMEM((8, rows), jnp.int32)],
        compiler_params=params(dimension_semantics=("arbitrary",)),
        cost_estimate=cost(2 * rows * width * slots, 2 * width * (rows + slots)),
        name="dispatch",
    )(dr, own)


def attend_kernel(held, *refs):
    q_ref, g_ref, own_ref, got_ref, wk_ref, wv_ref, entering_ref = refs[:7]
    o_ref, dq_ref, down_ref, sent_ref = refs[7 + held : 11 + held]
    kv_ref, s_ref, dp_ref, mem_t_ref, entering_t_ref = refs[11 + held :]
    readers = sent_ref.shape[0]
    dec = q_ref.shape[0]
    tile, width = own_ref.shape
    tiles = 1 + got_ref.shape[0] // tile
    lane = lax.broadcasted_iota(jnp.int32, (dec, PAIR), 1)
    q = q_ref[...] * jnp.asarray(SCALE, BF16)
    g = g_ref[...]
    zero = jnp.zeros_like(q)
    head = [lane < PAIR // 2, lane >= PAIR // 2]
    q_both = jnp.concatenate([jnp.where(head[h], q, zero) for h in range(2)], axis=0)
    g_both = jnp.concatenate([jnp.where(head[h], g, zero) for h in range(2)], axis=0)
    weights = jnp.concatenate([wk_ref[...], wv_ref[...]], axis=1)

    def frames(t):
        if t == 0:
            return own_ref[...]
        return got_ref[pl.ds((t - 1) * tile, tile), :width]

    @pl.when(pl.program_id(0) == 0)
    def _():
        for t in range(tiles):
            mem_t_ref[:, t * tile : (t + 1) * tile] = frames(t).T
        entering_t_ref[...] = entering_ref[...].T

    for t in range(tiles):
        kv_ref[pl.ds(t * tile, tile), :] = mm(frames(t), weights).astype(BF16)

    tops = []
    for t in range(tiles):
        at = pl.ds(t * tile, tile)
        s = mm(kv_ref[at, :PAIR], q_both, NT)
        if t > 0:
            flag = got_ref[pl.ds((t - 1) * tile, tile), width : width + PAIR]
            s = s + (flag.astype(F32)[:, 0:1] - 1.0) * 1e30
        s_ref[at, :] = s
        tops.append(jnp.max(s, axis=0, keepdims=True))
    top = functools.reduce(jnp.maximum, tops)
    total = jnp.zeros_like(top)
    inner = jnp.zeros_like(top)
    for t in range(tiles):
        at = pl.ds(t * tile, tile)
        e = jnp.exp(s_ref[at, :] - top)
        s_ref[at, :] = e
        total = total + jnp.sum(e, axis=0, keepdims=True)
        dp = mm(kv_ref[at, PAIR:], g_both, NT)
        dp_ref[at, :] = dp
        inner = inner + jnp.sum(e * dp, axis=0, keepdims=True)
    inverse = 1.0 / total
    inner = inner * inverse
    half = PAIR // 2
    out_t = [jnp.zeros((half, dec), F32) for _ in range(2)]
    dq_t = [jnp.zeros((half, dec), F32) for _ in range(2)]
    for t in range(tiles):
        at = pl.ds(t * tile, tile)
        kv_t = kv_ref[at, :].T
        p = s_ref[at, :] * inverse
        pb = p.astype(BF16)
        ds = (p * (dp_ref[at, :] - inner)).astype(BF16)
        for h in range(2):
            cols = slice(h * dec, (h + 1) * dec)
            dq_t[h] = dq_t[h] + mm(kv_t[h * half : (h + 1) * half], ds[:, cols])
            out_t[h] = out_t[h] + mm(kv_t[PAIR + h * half : PAIR + (h + 1) * half], pb[:, cols])
        dk = mm(ds, q_both)
        dv = mm(pb, g_both)
        dkv = jnp.concatenate([dk, dv], axis=1).astype(BF16)
        kv_ref[at, :] = dkv
        if t == 0:
            down_ref[...] = dkv
        else:
            count = tile // SLOTS
            dkv = dkv.reshape(count, SLOTS, 2 * PAIR)
            sent_ref[pl.ds((t - 1) * count, count), GRADS:, :] = dkv
    o_ref[...] = jnp.concatenate(out_t, axis=0).T.astype(BF16)
    dq = (jnp.concatenate(dq_t, axis=0) * SCALE).T.astype(BF16)
    dq_ref[...] = dq
    grad = mm(mem_t_ref[...], kv_ref[...]).reshape(readers, ROWS, 2 * PAIR)
    sent_ref[:, :ROWS, :] = grad.astype(BF16)
    grad = mm(entering_t_ref[...], dq).reshape(readers, ROWS, PAIR)
    grad = jnp.concatenate([grad[:, :TWICE], grad[:, ROWS - TWICE :]], axis=2)
    sent_ref[:, ROWS:GRADS, :] = grad.astype(BF16)


def attend(first, pairs, readers, queries, cot, own, got, wk, wv, entering, filled):
    dec, heads = queries.shape
    rows, width = own.shape
    slots = got.shape[0]
    total = rows + slots
    pair_at = lambda p: (0, first + p)
    whole = lambda p: (0, 0)
    return pl.pallas_call(
        functools.partial(attend_kernel, len(filled)),
        grid=(pairs,),
        in_specs=[
            pl.BlockSpec((dec, PAIR), pair_at),
            pl.BlockSpec((dec, PAIR), pair_at),
            pl.BlockSpec((rows, width), whole),
            pl.BlockSpec((slots, width + PAIR), whole),
            pl.BlockSpec((width, PAIR), pair_at),
            pl.BlockSpec((width, PAIR), pair_at),
            pl.BlockSpec((dec, width), whole),
        ]
        + [pl.BlockSpec(memory_space=pl.ANY)] * len(filled),
        out_specs=[
            pl.BlockSpec((dec, PAIR), pair_at),
            pl.BlockSpec((dec, PAIR), pair_at),
            pl.BlockSpec((rows, 2 * PAIR), pair_at),
            pl.BlockSpec((readers, SENT, 2 * PAIR), lambda p: (0, 0, p)),
        ],
        out_shape=(
            jax.ShapeDtypeStruct((dec, heads), BF16),
            jax.ShapeDtypeStruct((dec, heads), BF16),
            jax.ShapeDtypeStruct((rows, 2 * heads), BF16),
            jax.ShapeDtypeStruct((readers, SENT, 2 * PAIR * pairs), BF16),
        ),
        scratch_shapes=[
            pltpu.VMEM((total, 2 * PAIR), BF16),
            pltpu.VMEM((total, 2 * dec), F32),
            pltpu.VMEM((total, 2 * dec), F32),
            pltpu.VMEM((width, total), BF16),
            pltpu.VMEM((width, dec), BF16),
        ],
        input_output_aliases={7 + i: i for i in range(len(filled))},
        compiler_params=params(dimension_semantics=("arbitrary",)),
        cost_estimate=cost(
            pairs * (12 * dec * total * PAIR * 4 + 8 * width * total * PAIR),
            2 * total * width + pairs * 12 * total * PAIR,
            pairs * 2 * dec * total,
        ),
        name=f"attend_{first}",
    )(queries, cot, own, got, wk, wv, entering, *filled)


def query_kernel(dq_ref, wq_ref, dent_ref):
    dent_ref[...] = mm(dq_ref[...], wq_ref[...], NT).astype(BF16)


def query_side(dq, wq):
    dec = dq.shape[0]
    width, heads = wq.shape
    return pl.pallas_call(
        query_kernel,
        out_shape=jax.ShapeDtypeStruct((dec, width), BF16),
        compiler_params=params(),
        cost_estimate=cost(2 * dec * width * heads, 2 * width * (dec + heads)),
        name="query_side",
    )(dq, wq)


def table_kernel(capacity, dr_ref, out_ref):
    rows = out_ref.shape[0]
    slot_a, slot_b = slots_along_sublanes(dr_ref[...], capacity)
    for block in range(out_ref.shape[1] // rows):
        at = lax.broadcasted_iota(jnp.int32, (rows, rows), 1) + block * rows
        table = jnp.logical_or(at == slot_a, at == slot_b)
        out_ref[:, block * rows : (block + 1) * rows] = jnp.where(table, 1.0, 0.0).astype(BF16)


def table_of(capacity, readers, dr):
    shape = (dr.shape[1], readers * capacity)
    return pl.pallas_call(
        functools.partial(table_kernel, capacity),
        out_shape=jax.ShapeDtypeStruct(shape, BF16),
        compiler_params=params(),
        cost_estimate=cost(0, 2 * shape[0] * shape[1]),
        name="table_of",
    )(dr)


def combine_kernel(held, table_ref, down_ref, wk_ref, wv_ref, *refs):
    views = refs[: SLOTS // STEP]
    out_ref, sum_ref = refs[-2:]
    lanes = down_ref.shape[1]
    p = pl.program_id(0)
    back = jnp.concatenate([v[...] for v in views], axis=1).reshape(-1, lanes)
    tot = (down_ref[...].astype(F32) + mm(table_ref[...], back)).astype(BF16)
    weights = jnp.concatenate([wk_ref[...], wv_ref[...]], axis=1)
    out = mm(tot, weights, NT)

    @pl.when(p == 0)
    def _():
        sum_ref[...] = out + refs[SLOTS // STEP][...] if held else out

    @pl.when(p > 0)
    def _():
        sum_ref[...] += out

    @pl.when(p == pl.num_programs(0) - 1)
    def _():
        out_ref[...] = sum_ref[...].astype(out_ref.dtype)


def combine(first, last, table, down, back, wk, wv, held):
    rows = down.shape[0]
    width = wk.shape[0]
    readers, _, lanes = back.shape
    pairs = lanes // (2 * PAIR)
    whole = lambda p: (0, 0)
    pair_at = lambda p: (0, first + p)
    full = lambda a: pl.BlockSpec(a.shape, whole)
    view = lambda i: pl.BlockSpec((readers, STEP, 2 * PAIR), lambda p: (0, GRADS // STEP + i, p))
    return pl.pallas_call(
        functools.partial(combine_kernel, len(held)),
        grid=(pairs,),
        in_specs=[
            full(table),
            pl.BlockSpec((rows, 2 * PAIR), pair_at),
            pl.BlockSpec((width, PAIR), pair_at),
            pl.BlockSpec((width, PAIR), pair_at),
        ]
        + [view(i) for i in range(SLOTS // STEP)]
        + [full(h) for h in held],
        out_specs=pl.BlockSpec((rows, width), whole),
        out_shape=jax.ShapeDtypeStruct((rows, width), BF16 if last else F32),
        scratch_shapes=[pltpu.VMEM((rows, width), F32)],
        compiler_params=params(dimension_semantics=("arbitrary",)),
        cost_estimate=cost(
            2 * rows * lanes * (width + readers * SLOTS),
            2 * (rows * width + width * lanes + readers * SLOTS * lanes),
        ),
        name=f"combine_{first}",
    )(table, down, wk, wv, *([back] * (SLOTS // STEP)), *held)


def sum_kernel(last, back_ref, *refs):
    held, out_ref = refs[:-1], refs[-1]

    def added(lanes):
        sums = [back_ref[a, :, lanes].astype(F32) for a in range(4)]
        for a in range(4, back_ref.shape[0]):
            sums[a % 4] = sums[a % 4] + back_ref[a, :, lanes].astype(F32)
        return (sums[0] + sums[1]) + (sums[2] + sums[3])

    mine = [added(slice(c, c + PAIR)) for c in range(0, back_ref.shape[2], PAIR)]
    if not last:
        out_ref[...] = jnp.concatenate(mine, axis=1)
        return
    pieces = []
    for r in held:
        pieces += [r[:, c : c + PAIR] for c in range(0, r.shape[1], PAIR)]
    pieces += mine
    heads = out_ref.shape[1] // 3
    for p in range(heads // PAIR):
        upper, lower = pieces[2 * p], pieces[2 * p + 1]
        at = slice(p * PAIR, (p + 1) * PAIR)
        out_ref[:TWICE, at] = upper[ROWS:]
        out_ref[TWICE:, at] = lower[2 * TWICE :]
        out_ref[:, heads + p * PAIR : heads + (p + 1) * PAIR] = upper[:ROWS]
        out_ref[:, 2 * heads + p * PAIR : 2 * heads + (p + 1) * PAIR] = lower[:ROWS]


def summed(first, last, heads, back, held):
    readers, _, lanes = back.shape
    shape = (ROWS, 3 * heads) if last else (GRADS, lanes)
    whole = lambda i: (0, 0)
    return pl.pallas_call(
        functools.partial(sum_kernel, last),
        grid=(1,),
        in_specs=[pl.BlockSpec((readers, GRADS, lanes), lambda i: (0, 0, 0))]
        + [pl.BlockSpec(h.shape, whole) for h in held],
        out_specs=pl.BlockSpec(shape, whole),
        out_shape=jax.ShapeDtypeStruct(shape, F32),
        compiler_params=params(),
        cost_estimate=cost(readers * GRADS * lanes, 2 * readers * GRADS * lanes),
        name=f"summed_{first}",
    )(back, *held)


def per_device(encoder, destinations, hidden, w_query, w_key, w_value, cotangent):
    own = encoder[0, 0]
    dest = destinations[0, 0]
    wq, wk, wv = w_query[0], w_key[0], w_value[0]
    cot = cotangent[0, 0]
    rows, width = own.shape
    heads = wq.shape[1]
    readers = lax.axis_size("dp")
    capacity = 4 * rows // readers

    slots = readers * capacity

    slots = readers * capacity

    entering = passed_along(hidden[0, 0], "section", 1)
    out = dispatch(capacity, readers, dest.T, own)
    out, entering = lax.optimization_barrier((out, entering))
    queries = jnp.dot(entering, wq, preferred_element_type=F32).astype(BF16)
    got = exchanged(out.reshape(readers, capacity, -1)).reshape(slots, -1)

    filled, backs, firsts, first = (), [], [], 0
    for pairs in CHUNKS:
        *filled, sent = attend(
            first, pairs, readers, queries, cot, own, got, wk, wv, entering, filled
        )
        firsts.append(first)
        first += pairs
        backs.append(exchanged(sent))
    attended, dq, down = filled
    dentering = query_side(dq, wq)
    table = table_of(capacity, readers, dest.T)

    held, grads = [], []
    for c, first in enumerate(firsts):
        last = c == len(firsts) - 1
        if held:
            backs[c], held, grads, down, dentering, table = lax.optimization_barrier(
                (backs[c], held, grads, down, dentering, table)
            )
        if last:
            d_hidden = passed_along(dentering, "section", -1)
        held = [combine(first, last, table, down, backs[c], wk, wv, held)]
        grads.append(summed(first, last, heads, backs[c], grads))
    d_enc = held[0]
    grads = grads[-1]
    return (attended[None, None], d_hidden[None, None], d_enc[None, None], grads[None])


def solution(mesh):
    return jax.shard_map(
        per_device,
        mesh=mesh,
        in_specs=(
            P("dp", "section", None, None),
            P("dp", "section", None, None),
            P("dp", "section", None, None),
            P("section", None, None),
            P("section", None, None),
            P("section", None, None),
            P("dp", "section", None, None),
        ),
        out_specs=(
            P("dp", "section", None, None),
            P("dp", "section", None, None),
            P("dp", "section", None, None),
            P("section", "dp", None),
        ),
        check_vma=False,
    )
```

```python
import functools

import jax
import jax.numpy as jnp
from jax import lax
from jax.experimental import pallas as pl
from jax.experimental.pallas import tpu as pltpu
from jax.sharding import PartitionSpec as P

PAIR = 128
CHUNKS = (2, 3)
ROWS, TWICE, SLOTS = 40, 24, 48
GRADS = ROWS + TWICE
SENT = GRADS + SLOTS
STEP = 16
SCALE = 0.125
F32 = jnp.float32
BF16 = jnp.bfloat16
VMEM_LIMIT = 60 * 1024 * 1024
SMALL = 20 * 1024 * 1024

NT = (((1,), (1,)), ((), ()))
NN = (((1,), (0,)), ((), ()))


def mm(a, b, dims=NN):
    return lax.dot_general(a, b, dims, preferred_element_type=F32)


def params(grant=VMEM_LIMIT, **kw):
    return pltpu.CompilerParams(vmem_limit_bytes=grant, **kw)


def cost(flops, bytes_accessed, transcendentals=0):
    return pl.CostEstimate(
        flops=flops, bytes_accessed=bytes_accessed, transcendentals=transcendentals
    )


def passed_along(value, axis, steps):
    count = lax.axis_size(axis)
    pairs = [(source, (source + steps) % count) for source in range(count)]
    return lax.ppermute(value, axis, pairs)


def exchanged(value):
    return lax.all_to_all(value, "dp", split_axis=0, concat_axis=0, tiled=True)


def down_the_rows(dr):
    filler = jnp.zeros((8 - dr.shape[0], dr.shape[1]), F32)
    return jnp.concatenate([dr.astype(F32), filler], axis=0).T.astype(jnp.int32)


def slots_along_lanes(dr, capacity):
    dc = down_the_rows(dr)
    rows = dr.shape[1]
    shape = (rows, rows)
    before = lax.broadcasted_iota(jnp.int32, shape, 0) < lax.broadcasted_iota(
        jnp.int32, shape, 1
    )
    found = []
    for which in range(2):
        mine = dr[which : which + 1, :]
        same = jnp.logical_or(dc[:, 0:1] == mine, dc[:, 1:2] == mine)
        earlier = jnp.where(jnp.logical_and(same, before), 1.0, 0.0)
        place = jnp.sum(earlier, axis=0, keepdims=True).astype(jnp.int32)
        found.append(mine * capacity + place)
    return found


def slots_along_sublanes(dr, capacity):
    dc = down_the_rows(dr)
    rows = dr.shape[1]
    shape = (rows, rows)
    before = lax.broadcasted_iota(jnp.int32, shape, 1) < lax.broadcasted_iota(
        jnp.int32, shape, 0
    )
    found = []
    for which in range(2):
        mine = dc[:, which : which + 1]
        same = jnp.logical_or(dr[0:1, :] == mine, dr[1:2, :] == mine)
        earlier = jnp.where(jnp.logical_and(same, before), 1.0, 0.0)
        place = jnp.sum(earlier, axis=1, keepdims=True).astype(jnp.int32)
        found.append(mine * capacity + place)
    return found


def dispatch_kernel(capacity, dr_ref, own_ref, out_ref, slot_ref):
    rows = own_ref.shape[0]
    block = pl.program_id(0)

    @pl.when(block == 0)
    def _():
        for which, slot in enumerate(slots_along_lanes(dr_ref[...], capacity)):
            slot_ref[which : which + 1, :] = slot

    at = lax.broadcasted_iota(jnp.int32, (rows, rows), 0) + block * rows
    table = jnp.logical_or(at == slot_ref[0:1, :], at == slot_ref[1:2, :])
    table = jnp.where(table, 1.0, 0.0).astype(BF16)
    both = jnp.concatenate([own_ref[...], jnp.ones((rows, PAIR), BF16)], axis=1)
    out_ref[...] = mm(table, both).astype(BF16)


def dispatch(capacity, readers, dr, own):
    rows, width = own.shape
    slots = readers * capacity
    whole = lambda i: (0, 0)
    return pl.pallas_call(
        functools.partial(dispatch_kernel, capacity),
        grid=(slots // rows,),
        in_specs=[pl.BlockSpec(dr.shape, whole), pl.BlockSpec((rows, width), whole)],
        out_specs=pl.BlockSpec((rows, width + PAIR), lambda i: (i, 0)),
        out_shape=jax.ShapeDtypeStruct((slots, width + PAIR), BF16),
        scratch_shapes=[pltpu.VMEM((8, rows), jnp.int32)],
        compiler_params=params(dimension_semantics=("arbitrary",)),
        cost_estimate=cost(2 * rows * width * slots, 2 * width * (rows + slots)),
        name="dispatch",
    )(dr, own)


def attend_kernel(held, *refs):
    q_ref, g_ref, own_ref, got_ref, wk_ref, wv_ref, entering_ref = refs[:7]
    o_ref, dq_ref, down_ref, sent_ref = refs[7 + held : 11 + held]
    kv_ref, s_ref, dp_ref, mem_t_ref, entering_t_ref = refs[11 + held :]
    readers = sent_ref.shape[0]
    dec = q_ref.shape[0]
    tile, width = own_ref.shape
    tiles = 1 + got_ref.shape[0] // tile
    lane = lax.broadcasted_iota(jnp.int32, (dec, PAIR), 1)
    q = q_ref[...] * jnp.asarray(SCALE, BF16)
    g = g_ref[...]
    zero = jnp.zeros_like(q)
    head = [lane < PAIR // 2, lane >= PAIR // 2]
    q_both = jnp.concatenate([jnp.where(head[h], q, zero) for h in range(2)], axis=0)
    g_both = jnp.concatenate([jnp.where(head[h], g, zero) for h in range(2)], axis=0)
    weights = jnp.concatenate([wk_ref[...], wv_ref[...]], axis=1)

    def frames(t):
        if t == 0:
            return own_ref[...]
        return got_ref[pl.ds((t - 1) * tile, tile), :width]

    @pl.when(pl.program_id(0) == 0)
    def _():
        for t in range(tiles):
            mem_t_ref[:, t * tile : (t + 1) * tile] = frames(t).T
        entering_t_ref[...] = entering_ref[...].T

    for t in range(tiles):
        kv_ref[pl.ds(t * tile, tile), :] = mm(frames(t), weights).astype(BF16)

    tops = []
    for t in range(tiles):
        at = pl.ds(t * tile, tile)
        s = mm(kv_ref[at, :PAIR], q_both, NT)
        if t > 0:
            flag = got_ref[pl.ds((t - 1) * tile, tile), width : width + PAIR]
            s = s + (flag.astype(F32)[:, 0:1] - 1.0) * 1e30
        s_ref[at, :] = s
        tops.append(jnp.max(s, axis=0, keepdims=True))
    top = functools.reduce(jnp.maximum, tops)
    total = jnp.zeros_like(top)
    inner = jnp.zeros_like(top)
    for t in range(tiles):
        at = pl.ds(t * tile, tile)
        e = jnp.exp(s_ref[at, :] - top)
        s_ref[at, :] = e
        total = total + jnp.sum(e, axis=0, keepdims=True)
        dp = mm(kv_ref[at, PAIR:], g_both, NT)
        dp_ref[at, :] = dp
        inner = inner + jnp.sum(e * dp, axis=0, keepdims=True)
    inverse = 1.0 / total
    inner = inner * inverse
    half = PAIR // 2
    out_t = [jnp.zeros((half, dec), F32) for _ in range(2)]
    dq_t = [jnp.zeros((half, dec), F32) for _ in range(2)]
    for t in range(tiles):
        at = pl.ds(t * tile, tile)
        kv_t = kv_ref[at, :].T
        p = s_ref[at, :] * inverse
        pb = p.astype(BF16)
        ds = (p * (dp_ref[at, :] - inner)).astype(BF16)
        for h in range(2):
            cols = slice(h * dec, (h + 1) * dec)
            dq_t[h] = dq_t[h] + mm(kv_t[h * half : (h + 1) * half], ds[:, cols])
            out_t[h] = out_t[h] + mm(kv_t[PAIR + h * half : PAIR + (h + 1) * half], pb[:, cols])
        dk = mm(ds, q_both)
        dv = mm(pb, g_both)
        dkv = jnp.concatenate([dk, dv], axis=1).astype(BF16)
        kv_ref[at, :] = dkv
        if t == 0:
            down_ref[...] = dkv
        else:
            count = tile // SLOTS
            dkv = dkv.reshape(count, SLOTS, 2 * PAIR)
            sent_ref[pl.ds((t - 1) * count, count), GRADS:, :] = dkv
    o_ref[...] = jnp.concatenate(out_t, axis=0).T.astype(BF16)
    dq = (jnp.concatenate(dq_t, axis=0) * SCALE).T.astype(BF16)
    dq_ref[...] = dq
    grad = mm(mem_t_ref[...], kv_ref[...]).reshape(readers, ROWS, 2 * PAIR)
    sent_ref[:, :ROWS, :] = grad.astype(BF16)
    grad = mm(entering_t_ref[...], dq).reshape(readers, ROWS, PAIR)
    grad = jnp.concatenate([grad[:, :TWICE], grad[:, ROWS - TWICE :]], axis=2)
    sent_ref[:, ROWS:GRADS, :] = grad.astype(BF16)


def attend(first, pairs, readers, queries, cot, own, got, wk, wv, entering, filled):
    dec, heads = queries.shape
    rows, width = own.shape
    slots = got.shape[0]
    total = rows + slots
    pair_at = lambda p: (0, first + p)
    whole = lambda p: (0, 0)
    return pl.pallas_call(
        functools.partial(attend_kernel, len(filled)),
        grid=(pairs,),
        in_specs=[
            pl.BlockSpec((dec, PAIR), pair_at),
            pl.BlockSpec((dec, PAIR), pair_at),
            pl.BlockSpec((rows, width), whole),
            pl.BlockSpec((slots, width + PAIR), whole),
            pl.BlockSpec((width, PAIR), pair_at),
            pl.BlockSpec((width, PAIR), pair_at),
            pl.BlockSpec((dec, width), whole),
        ]
        + [pl.BlockSpec(memory_space=pl.ANY)] * len(filled),
        out_specs=[
            pl.BlockSpec((dec, PAIR), pair_at),
            pl.BlockSpec((dec, PAIR), pair_at),
            pl.BlockSpec((rows, 2 * PAIR), pair_at),
            pl.BlockSpec((readers, SENT, 2 * PAIR), lambda p: (0, 0, p)),
        ],
        out_shape=(
            jax.ShapeDtypeStruct((dec, heads), BF16),
            jax.ShapeDtypeStruct((dec, heads), BF16),
            jax.ShapeDtypeStruct((rows, 2 * heads), BF16),
            jax.ShapeDtypeStruct((readers, SENT, 2 * PAIR * pairs), BF16),
        ),
        scratch_shapes=[
            pltpu.VMEM((total, 2 * PAIR), BF16),
            pltpu.VMEM((total, 2 * dec), F32),
            pltpu.VMEM((total, 2 * dec), F32),
            pltpu.VMEM((width, total), BF16),
            pltpu.VMEM((width, dec), BF16),
        ],
        input_output_aliases={7 + i: i for i in range(len(filled))},
        compiler_params=params(dimension_semantics=("arbitrary",)),
        cost_estimate=cost(
            pairs * (12 * dec * total * PAIR * 4 + 8 * width * total * PAIR),
            2 * total * width + pairs * 12 * total * PAIR,
            pairs * 2 * dec * total,
        ),
        name=f"attend_{first}",
    )(queries, cot, own, got, wk, wv, entering, *filled)


def query_kernel(dq_ref, wq_ref, dent_ref):
    dent_ref[...] = mm(dq_ref[...], wq_ref[...], NT).astype(BF16)


def query_side(dq, wq):
    dec = dq.shape[0]
    width, heads = wq.shape
    return pl.pallas_call(
        query_kernel,
        out_shape=jax.ShapeDtypeStruct((dec, width), BF16),
        compiler_params=params(SMALL),
        cost_estimate=cost(2 * dec * width * heads, 2 * width * (dec + heads)),
        name="query_side",
    )(dq, wq)


def table_kernel(capacity, dr_ref, out_ref):
    rows = out_ref.shape[0]
    slot_a, slot_b = slots_along_sublanes(dr_ref[...], capacity)
    for block in range(out_ref.shape[1] // rows):
        at = lax.broadcasted_iota(jnp.int32, (rows, rows), 1) + block * rows
        table = jnp.logical_or(at == slot_a, at == slot_b)
        out_ref[:, block * rows : (block + 1) * rows] = jnp.where(table, 1.0, 0.0).astype(BF16)


def table_of(capacity, readers, dr):
    shape = (dr.shape[1], readers * capacity)
    return pl.pallas_call(
        functools.partial(table_kernel, capacity),
        out_shape=jax.ShapeDtypeStruct(shape, BF16),
        compiler_params=params(SMALL),
        cost_estimate=cost(0, 2 * shape[0] * shape[1]),
        name="table_of",
    )(dr)


def combine_kernel(held, table_ref, down_ref, wk_ref, wv_ref, *refs):
    views = refs[: SLOTS // STEP]
    out_ref, sum_ref = refs[-2:]
    lanes = down_ref.shape[1]
    p = pl.program_id(0)
    back = jnp.concatenate([v[...] for v in views], axis=1).reshape(-1, lanes)
    tot = (down_ref[...].astype(F32) + mm(table_ref[...], back)).astype(BF16)
    weights = jnp.concatenate([wk_ref[...], wv_ref[...]], axis=1)
    out = mm(tot, weights, NT)

    @pl.when(p == 0)
    def _():
        sum_ref[...] = out + refs[SLOTS // STEP][...] if held else out

    @pl.when(p > 0)
    def _():
        sum_ref[...] += out

    @pl.when(p == pl.num_programs(0) - 1)
    def _():
        out_ref[...] = sum_ref[...].astype(out_ref.dtype)


def combine(first, last, table, down, back, wk, wv, held):
    rows = down.shape[0]
    width = wk.shape[0]
    readers, _, lanes = back.shape
    pairs = lanes // (2 * PAIR)
    whole = lambda p: (0, 0)
    pair_at = lambda p: (0, first + p)
    full = lambda a: pl.BlockSpec(a.shape, whole)
    view = lambda i: pl.BlockSpec((readers, STEP, 2 * PAIR), lambda p: (0, GRADS // STEP + i, p))
    return pl.pallas_call(
        functools.partial(combine_kernel, len(held)),
        grid=(pairs,),
        in_specs=[
            full(table),
            pl.BlockSpec((rows, 2 * PAIR), pair_at),
            pl.BlockSpec((width, PAIR), pair_at),
            pl.BlockSpec((width, PAIR), pair_at),
        ]
        + [view(i) for i in range(SLOTS // STEP)]
        + [full(h) for h in held],
        out_specs=pl.BlockSpec((rows, width), whole),
        out_shape=jax.ShapeDtypeStruct((rows, width), BF16 if last else F32),
        scratch_shapes=[pltpu.VMEM((rows, width), F32)],
        compiler_params=params(SMALL, dimension_semantics=("arbitrary",)),
        cost_estimate=cost(
            2 * rows * lanes * (width + readers * SLOTS),
            2 * (rows * width + width * lanes + readers * SLOTS * lanes),
        ),
        name=f"combine_{first}",
    )(table, down, wk, wv, *([back] * (SLOTS // STEP)), *held)


def sum_kernel(last, back_ref, *refs):
    held, out_ref = refs[:-1], refs[-1]

    def added(lanes):
        sums = [back_ref[a, :, lanes].astype(F32) for a in range(4)]
        for a in range(4, back_ref.shape[0]):
            sums[a % 4] = sums[a % 4] + back_ref[a, :, lanes].astype(F32)
        return (sums[0] + sums[1]) + (sums[2] + sums[3])

    mine = [added(slice(c, c + PAIR)) for c in range(0, back_ref.shape[2], PAIR)]
    if not last:
        out_ref[...] = jnp.concatenate(mine, axis=1)
        return
    pieces = []
    for r in held:
        pieces += [r[:, c : c + PAIR] for c in range(0, r.shape[1], PAIR)]
    pieces += mine
    heads = out_ref.shape[1] // 3
    for p in range(heads // PAIR):
        upper, lower = pieces[2 * p], pieces[2 * p + 1]
        at = slice(p * PAIR, (p + 1) * PAIR)
        out_ref[:TWICE, at] = upper[ROWS:]
        out_ref[TWICE:, at] = lower[2 * TWICE :]
        out_ref[:, heads + p * PAIR : heads + (p + 1) * PAIR] = upper[:ROWS]
        out_ref[:, 2 * heads + p * PAIR : 2 * heads + (p + 1) * PAIR] = lower[:ROWS]


def summed(first, last, heads, back, held):
    readers, _, lanes = back.shape
    shape = (ROWS, 3 * heads) if last else (GRADS, lanes)
    whole = lambda i: (0, 0)
    return pl.pallas_call(
        functools.partial(sum_kernel, last),
        grid=(1,),
        in_specs=[pl.BlockSpec((readers, GRADS, lanes), lambda i: (0, 0, 0))]
        + [pl.BlockSpec(h.shape, whole) for h in held],
        out_specs=pl.BlockSpec(shape, whole),
        out_shape=jax.ShapeDtypeStruct(shape, F32),
        compiler_params=params(SMALL),
        cost_estimate=cost(readers * GRADS * lanes, 2 * readers * GRADS * lanes),
        name=f"summed_{first}",
    )(back, *held)


def per_device(encoder, destinations, hidden, w_query, w_key, w_value, cotangent):
    own = encoder[0, 0]
    dest = destinations[0, 0]
    wq, wk, wv = w_query[0], w_key[0], w_value[0]
    cot = cotangent[0, 0]
    rows, width = own.shape
    heads = wq.shape[1]
    readers = lax.axis_size("dp")
    capacity = 4 * rows // readers

    slots = readers * capacity

    slots = readers * capacity

    entering = passed_along(hidden[0, 0], "section", 1)
    out = dispatch(capacity, readers, dest.T, own)
    queries = jnp.dot(entering, wq, preferred_element_type=F32).astype(BF16)
    got = exchanged(out.reshape(readers, capacity, -1)).reshape(slots, -1)

    filled, backs, firsts, first = (), [], [], 0
    for pairs in CHUNKS:
        *filled, sent = attend(
            first, pairs, readers, queries, cot, own, got, wk, wv, entering, filled
        )
        firsts.append(first)
        first += pairs
        backs.append(exchanged(sent))
    attended, dq, down = filled
    dentering = query_side(dq, wq)
    table = table_of(capacity, readers, dest.T)

    held, grads = [], []
    for c, first in enumerate(firsts):
        last = c == len(firsts) - 1
        if held:
            backs[c], held, grads, down, dentering, table = lax.optimization_barrier(
                (backs[c], held, grads, down, dentering, table)
            )
        if last:
            d_hidden = passed_along(dentering, "section", -1)
        held = [combine(first, last, table, down, backs[c], wk, wv, held)]
        grads.append(summed(first, last, heads, backs[c], grads))
    d_enc = held[0]
    grads = grads[-1]
    return (attended[None, None], d_hidden[None, None], d_enc[None, None], grads[None])


def solution(mesh):
    return jax.shard_map(
        per_device,
        mesh=mesh,
        in_specs=(
            P("dp", "section", None, None),
            P("dp", "section", None, None),
            P("dp", "section", None, None),
            P("section", None, None),
            P("section", None, None),
            P("section", None, None),
            P("dp", "section", None, None),
        ),
        out_specs=(
            P("dp", "section", None, None),
            P("dp", "section", None, None),
            P("dp", "section", None, None),
            P("section", "dp", None),
        ),
        check_vma=False,
    )
```

```python
import functools

import jax
import jax.numpy as jnp
from jax import lax
from jax.experimental import pallas as pl
from jax.experimental.pallas import tpu as pltpu
from jax.sharding import PartitionSpec as P

PAIR = 128
CHUNKS = (2, 3)
ROWS, TWICE, SLOTS = 40, 24, 48
GRADS = ROWS + TWICE
SENT = GRADS + SLOTS
STEP = 16
SCALE = 0.125
F32 = jnp.float32
BF16 = jnp.bfloat16
VMEM_LIMIT = 60 * 1024 * 1024
SMALL = 20 * 1024 * 1024

NT = (((1,), (1,)), ((), ()))
NN = (((1,), (0,)), ((), ()))


def mm(a, b, dims=NN):
    return lax.dot_general(a, b, dims, preferred_element_type=F32)


def params(grant=VMEM_LIMIT, **kw):
    return pltpu.CompilerParams(vmem_limit_bytes=grant, **kw)


def cost(flops, bytes_accessed, transcendentals=0):
    return pl.CostEstimate(
        flops=flops, bytes_accessed=bytes_accessed, transcendentals=transcendentals
    )


def passed_along(value, axis, steps):
    count = lax.axis_size(axis)
    pairs = [(source, (source + steps) % count) for source in range(count)]
    return lax.ppermute(value, axis, pairs)


def exchanged(value):
    return lax.all_to_all(value, "dp", split_axis=0, concat_axis=0, tiled=True)


def down_the_rows(dr):
    filler = jnp.zeros((8 - dr.shape[0], dr.shape[1]), F32)
    return jnp.concatenate([dr.astype(F32), filler], axis=0).T.astype(jnp.int32)


def slots_along_lanes(dr, capacity):
    dc = down_the_rows(dr)
    rows = dr.shape[1]
    shape = (rows, rows)
    before = lax.broadcasted_iota(jnp.int32, shape, 0) < lax.broadcasted_iota(
        jnp.int32, shape, 1
    )
    found = []
    for which in range(2):
        mine = dr[which : which + 1, :]
        same = jnp.logical_or(dc[:, 0:1] == mine, dc[:, 1:2] == mine)
        earlier = jnp.where(jnp.logical_and(same, before), 1.0, 0.0)
        place = jnp.sum(earlier, axis=0, keepdims=True).astype(jnp.int32)
        found.append(mine * capacity + place)
    return found


def slots_along_sublanes(dr, capacity):
    dc = down_the_rows(dr)
    rows = dr.shape[1]
    shape = (rows, rows)
    before = lax.broadcasted_iota(jnp.int32, shape, 1) < lax.broadcasted_iota(
        jnp.int32, shape, 0
    )
    found = []
    for which in range(2):
        mine = dc[:, which : which + 1]
        same = jnp.logical_or(dr[0:1, :] == mine, dr[1:2, :] == mine)
        earlier = jnp.where(jnp.logical_and(same, before), 1.0, 0.0)
        place = jnp.sum(earlier, axis=1, keepdims=True).astype(jnp.int32)
        found.append(mine * capacity + place)
    return found


def dispatch_kernel(capacity, dr_ref, own_ref, out_ref, slot_ref):
    rows = own_ref.shape[0]
    block = pl.program_id(0)

    @pl.when(block == 0)
    def _():
        for which, slot in enumerate(slots_along_lanes(dr_ref[...], capacity)):
            slot_ref[which : which + 1, :] = slot

    at = lax.broadcasted_iota(jnp.int32, (rows, rows), 0) + block * rows
    table = jnp.logical_or(at == slot_ref[0:1, :], at == slot_ref[1:2, :])
    table = jnp.where(table, 1.0, 0.0).astype(BF16)
    both = jnp.concatenate([own_ref[...], jnp.ones((rows, PAIR), BF16)], axis=1)
    out_ref[...] = mm(table, both).astype(BF16)


def dispatch(capacity, readers, dr, own):
    rows, width = own.shape
    slots = readers * capacity
    whole = lambda i: (0, 0)
    return pl.pallas_call(
        functools.partial(dispatch_kernel, capacity),
        grid=(slots // rows,),
        in_specs=[pl.BlockSpec(dr.shape, whole), pl.BlockSpec((rows, width), whole)],
        out_specs=pl.BlockSpec((rows, width + PAIR), lambda i: (i, 0)),
        out_shape=jax.ShapeDtypeStruct((slots, width + PAIR), BF16),
        scratch_shapes=[pltpu.VMEM((8, rows), jnp.int32)],
        compiler_params=params(dimension_semantics=("arbitrary",)),
        cost_estimate=cost(2 * rows * width * slots, 2 * width * (rows + slots)),
        name="dispatch",
    )(dr, own)


def attend_kernel(held, *refs):
    q_ref, g_ref, own_ref, got_ref, wk_ref, wv_ref, entering_ref = refs[:7]
    o_ref, dq_ref, down_ref, sent_ref = refs[7 + held : 11 + held]
    kv_ref, s_ref, dp_ref, mem_t_ref, entering_t_ref = refs[11 + held :]
    readers = sent_ref.shape[0]
    dec = q_ref.shape[0]
    tile, width = own_ref.shape
    tiles = 1 + got_ref.shape[0] // tile
    lane = lax.broadcasted_iota(jnp.int32, (dec, PAIR), 1)
    q = q_ref[...] * jnp.asarray(SCALE, BF16)
    g = g_ref[...]
    zero = jnp.zeros_like(q)
    head = [lane < PAIR // 2, lane >= PAIR // 2]
    q_both = jnp.concatenate([jnp.where(head[h], q, zero) for h in range(2)], axis=0)
    g_both = jnp.concatenate([jnp.where(head[h], g, zero) for h in range(2)], axis=0)
    weights = jnp.concatenate([wk_ref[...], wv_ref[...]], axis=1)

    def frames(t):
        if t == 0:
            return own_ref[...]
        return got_ref[pl.ds((t - 1) * tile, tile), :width]

    @pl.when(pl.program_id(0) == 0)
    def _():
        for t in range(tiles):
            mem_t_ref[:, t * tile : (t + 1) * tile] = frames(t).T
        entering_t_ref[...] = entering_ref[...].T

    for t in range(tiles):
        kv_ref[pl.ds(t * tile, tile), :] = mm(frames(t), weights).astype(BF16)

    tops = []
    for t in range(tiles):
        at = pl.ds(t * tile, tile)
        s = mm(kv_ref[at, :PAIR], q_both, NT)
        if t > 0:
            flag = got_ref[pl.ds((t - 1) * tile, tile), width : width + PAIR]
            s = s + (flag.astype(F32)[:, 0:1] - 1.0) * 1e30
        s_ref[at, :] = s
        tops.append(jnp.max(s, axis=0, keepdims=True))
    top = functools.reduce(jnp.maximum, tops)
    total = jnp.zeros_like(top)
    inner = jnp.zeros_like(top)
    for t in range(tiles):
        at = pl.ds(t * tile, tile)
        e = jnp.exp(s_ref[at, :] - top)
        s_ref[at, :] = e
        total = total + jnp.sum(e, axis=0, keepdims=True)
        dp = mm(kv_ref[at, PAIR:], g_both, NT)
        dp_ref[at, :] = dp
        inner = inner + jnp.sum(e * dp, axis=0, keepdims=True)
    inverse = 1.0 / total
    inner = inner * inverse
    half = PAIR // 2
    out_t = [jnp.zeros((half, dec), F32) for _ in range(2)]
    dq_t = [jnp.zeros((half, dec), F32) for _ in range(2)]
    for t in range(tiles):
        at = pl.ds(t * tile, tile)
        kv_t = kv_ref[at, :].T
        p = s_ref[at, :] * inverse
        pb = p.astype(BF16)
        ds = (p * (dp_ref[at, :] - inner)).astype(BF16)
        for h in range(2):
            cols = slice(h * dec, (h + 1) * dec)
            dq_t[h] = dq_t[h] + mm(kv_t[h * half : (h + 1) * half], ds[:, cols])
            out_t[h] = out_t[h] + mm(kv_t[PAIR + h * half : PAIR + (h + 1) * half], pb[:, cols])
        dk = mm(ds, q_both)
        dv = mm(pb, g_both)
        dkv = jnp.concatenate([dk, dv], axis=1).astype(BF16)
        kv_ref[at, :] = dkv
        if t == 0:
            down_ref[...] = dkv
        else:
            count = tile // SLOTS
            dkv = dkv.reshape(count, SLOTS, 2 * PAIR)
            sent_ref[pl.ds((t - 1) * count, count), GRADS:, :] = dkv
    o_ref[...] = jnp.concatenate(out_t, axis=0).T.astype(BF16)
    dq = (jnp.concatenate(dq_t, axis=0) * SCALE).T.astype(BF16)
    dq_ref[...] = dq
    grad = mm(mem_t_ref[...], kv_ref[...]).reshape(readers, ROWS, 2 * PAIR)
    sent_ref[:, :ROWS, :] = grad.astype(BF16)
    grad = mm(entering_t_ref[...], dq).reshape(readers, ROWS, PAIR)
    grad = jnp.concatenate([grad[:, :TWICE], grad[:, ROWS - TWICE :]], axis=2)
    sent_ref[:, ROWS:GRADS, :] = grad.astype(BF16)


def attend(first, pairs, readers, queries, cot, own, got, wk, wv, entering, filled):
    dec, heads = queries.shape
    rows, width = own.shape
    slots = got.shape[0]
    total = rows + slots
    pair_at = lambda p: (0, first + p)
    whole = lambda p: (0, 0)
    return pl.pallas_call(
        functools.partial(attend_kernel, len(filled)),
        grid=(pairs,),
        in_specs=[
            pl.BlockSpec((dec, PAIR), pair_at),
            pl.BlockSpec((dec, PAIR), pair_at),
            pl.BlockSpec((rows, width), whole),
            pl.BlockSpec((slots, width + PAIR), whole),
            pl.BlockSpec((width, PAIR), pair_at),
            pl.BlockSpec((width, PAIR), pair_at),
            pl.BlockSpec((dec, width), whole),
        ]
        + [pl.BlockSpec(memory_space=pl.ANY)] * len(filled),
        out_specs=[
            pl.BlockSpec((dec, PAIR), pair_at),
            pl.BlockSpec((dec, PAIR), pair_at),
            pl.BlockSpec((rows, 2 * PAIR), pair_at),
            pl.BlockSpec((readers, SENT, 2 * PAIR), lambda p: (0, 0, p)),
        ],
        out_shape=(
            jax.ShapeDtypeStruct((dec, heads), BF16),
            jax.ShapeDtypeStruct((dec, heads), BF16),
            jax.ShapeDtypeStruct((rows, 2 * heads), BF16),
            jax.ShapeDtypeStruct((readers, SENT, 2 * PAIR * pairs), BF16),
        ),
        scratch_shapes=[
            pltpu.VMEM((total, 2 * PAIR), BF16),
            pltpu.VMEM((total, 2 * dec), F32),
            pltpu.VMEM((total, 2 * dec), F32),
            pltpu.VMEM((width, total), BF16),
            pltpu.VMEM((width, dec), BF16),
        ],
        input_output_aliases={7 + i: i for i in range(len(filled))},
        compiler_params=params(dimension_semantics=("arbitrary",)),
        cost_estimate=cost(
            pairs * (12 * dec * total * PAIR * 4 + 8 * width * total * PAIR),
            2 * total * width + pairs * 12 * total * PAIR,
            pairs * 2 * dec * total,
        ),
        name=f"attend_{first}",
    )(queries, cot, own, got, wk, wv, entering, *filled)


def query_kernel(dq_ref, wq_ref, dent_ref):
    dent_ref[...] = mm(dq_ref[...], wq_ref[...], NT).astype(BF16)


def query_side(dq, wq):
    dec = dq.shape[0]
    width, heads = wq.shape
    return pl.pallas_call(
        query_kernel,
        out_shape=jax.ShapeDtypeStruct((dec, width), BF16),
        compiler_params=params(SMALL),
        cost_estimate=cost(2 * dec * width * heads, 2 * width * (dec + heads)),
        name="query_side",
    )(dq, wq)


def table_kernel(capacity, dr_ref, out_ref):
    rows = out_ref.shape[0]
    slot_a, slot_b = slots_along_sublanes(dr_ref[...], capacity)
    for block in range(out_ref.shape[1] // rows):
        at = lax.broadcasted_iota(jnp.int32, (rows, rows), 1) + block * rows
        table = jnp.logical_or(at == slot_a, at == slot_b)
        out_ref[:, block * rows : (block + 1) * rows] = jnp.where(table, 1.0, 0.0).astype(BF16)


def table_of(capacity, readers, dr):
    shape = (dr.shape[1], readers * capacity)
    return pl.pallas_call(
        functools.partial(table_kernel, capacity),
        out_shape=jax.ShapeDtypeStruct(shape, BF16),
        compiler_params=params(SMALL),
        cost_estimate=cost(0, 2 * shape[0] * shape[1]),
        name="table_of",
    )(dr)


def combine_kernel(held, table_ref, down_ref, wk_ref, wv_ref, *refs):
    views = refs[: SLOTS // STEP]
    out_ref, sum_ref = refs[-2:]
    lanes = down_ref.shape[1]
    p = pl.program_id(0)
    back = jnp.concatenate([v[...] for v in views], axis=1).reshape(-1, lanes)
    tot = (down_ref[...].astype(F32) + mm(table_ref[...], back)).astype(BF16)
    weights = jnp.concatenate([wk_ref[...], wv_ref[...]], axis=1)
    out = mm(tot, weights, NT)

    @pl.when(p == 0)
    def _():
        sum_ref[...] = out + refs[SLOTS // STEP][...] if held else out

    @pl.when(p > 0)
    def _():
        sum_ref[...] += out

    @pl.when(p == pl.num_programs(0) - 1)
    def _():
        out_ref[...] = sum_ref[...].astype(out_ref.dtype)


def combine(first, last, table, down, back, wk, wv, held):
    rows = down.shape[0]
    width = wk.shape[0]
    readers, _, lanes = back.shape
    pairs = lanes // (2 * PAIR)
    whole = lambda p: (0, 0)
    pair_at = lambda p: (0, first + p)
    full = lambda a: pl.BlockSpec(a.shape, whole)
    view = lambda i: pl.BlockSpec((readers, STEP, 2 * PAIR), lambda p: (0, GRADS // STEP + i, p))
    return pl.pallas_call(
        functools.partial(combine_kernel, len(held)),
        grid=(pairs,),
        in_specs=[
            full(table),
            pl.BlockSpec((rows, 2 * PAIR), pair_at),
            pl.BlockSpec((width, PAIR), pair_at),
            pl.BlockSpec((width, PAIR), pair_at),
        ]
        + [view(i) for i in range(SLOTS // STEP)]
        + [full(h) for h in held],
        out_specs=pl.BlockSpec((rows, width), whole),
        out_shape=jax.ShapeDtypeStruct((rows, width), BF16 if last else F32),
        scratch_shapes=[pltpu.VMEM((rows, width), F32)],
        compiler_params=params(SMALL, dimension_semantics=("arbitrary",)),
        cost_estimate=cost(
            2 * rows * lanes * (width + readers * SLOTS),
            2 * (rows * width + width * lanes + readers * SLOTS * lanes),
        ),
        name=f"combine_{first}",
    )(table, down, wk, wv, *([back] * (SLOTS // STEP)), *held)


def sum_kernel(last, back_ref, *refs):
    held, out_ref = refs[:-1], refs[-1]

    def added(lanes):
        sums = [back_ref[a, :, lanes].astype(F32) for a in range(4)]
        for a in range(4, back_ref.shape[0]):
            sums[a % 4] = sums[a % 4] + back_ref[a, :, lanes].astype(F32)
        return (sums[0] + sums[1]) + (sums[2] + sums[3])

    mine = [added(slice(c, c + PAIR)) for c in range(0, back_ref.shape[2], PAIR)]
    if not last:
        out_ref[...] = jnp.concatenate(mine, axis=1)
        return
    pieces = []
    for r in held:
        pieces += [r[:, c : c + PAIR] for c in range(0, r.shape[1], PAIR)]
    pieces += mine
    heads = out_ref.shape[1] // 3
    for p in range(heads // PAIR):
        upper, lower = pieces[2 * p], pieces[2 * p + 1]
        at = slice(p * PAIR, (p + 1) * PAIR)
        out_ref[:TWICE, at] = upper[ROWS:]
        out_ref[TWICE:, at] = lower[2 * TWICE :]
        out_ref[:, heads + p * PAIR : heads + (p + 1) * PAIR] = upper[:ROWS]
        out_ref[:, 2 * heads + p * PAIR : 2 * heads + (p + 1) * PAIR] = lower[:ROWS]


def summed(first, last, heads, back, held):
    readers, _, lanes = back.shape
    shape = (ROWS, 3 * heads) if last else (GRADS, lanes)
    whole = lambda i: (0, 0)
    return pl.pallas_call(
        functools.partial(sum_kernel, last),
        grid=(1,),
        in_specs=[pl.BlockSpec((readers, GRADS, lanes), lambda i: (0, 0, 0))]
        + [pl.BlockSpec(h.shape, whole) for h in held],
        out_specs=pl.BlockSpec(shape, whole),
        out_shape=jax.ShapeDtypeStruct(shape, F32),
        compiler_params=params(SMALL),
        cost_estimate=cost(readers * GRADS * lanes, 2 * readers * GRADS * lanes),
        name=f"summed_{first}",
    )(back, *held)


def per_device(encoder, destinations, hidden, w_query, w_key, w_value, cotangent):
    own = encoder[0, 0]
    dest = destinations[0, 0]
    wq, wk, wv = w_query[0], w_key[0], w_value[0]
    cot = cotangent[0, 0]
    rows, width = own.shape
    heads = wq.shape[1]
    readers = lax.axis_size("dp")
    capacity = 4 * rows // readers

    slots = readers * capacity

    slots = readers * capacity

    entering = passed_along(hidden[0, 0], "section", 1)
    out = dispatch(capacity, readers, dest.T, own)
    out, entering = lax.optimization_barrier((out, entering))
    queries = jnp.dot(entering, wq, preferred_element_type=F32).astype(BF16)
    got = exchanged(out.reshape(readers, capacity, -1)).reshape(slots, -1)

    filled, backs, firsts, first = (), [], [], 0
    for pairs in CHUNKS:
        *filled, sent = attend(
            first, pairs, readers, queries, cot, own, got, wk, wv, entering, filled
        )
        firsts.append(first)
        first += pairs
        backs.append(exchanged(sent))
    attended, dq, down = filled
    dentering = query_side(dq, wq)
    table = table_of(capacity, readers, dest.T)

    held, grads = [], []
    for c, first in enumerate(firsts):
        last = c == len(firsts) - 1
        if held:
            backs[c], held, grads, down, dentering, table = lax.optimization_barrier(
                (backs[c], held, grads, down, dentering, table)
            )
        if last:
            d_hidden = passed_along(dentering, "section", -1)
        held = [combine(first, last, table, down, backs[c], wk, wv, held)]
        grads.append(summed(first, last, heads, backs[c], grads))
    d_enc = held[0]
    grads = grads[-1]
    return (attended[None, None], d_hidden[None, None], d_enc[None, None], grads[None])


def solution(mesh):
    return jax.shard_map(
        per_device,
        mesh=mesh,
        in_specs=(
            P("dp", "section", None, None),
            P("dp", "section", None, None),
            P("dp", "section", None, None),
            P("section", None, None),
            P("section", None, None),
            P("section", None, None),
            P("dp", "section", None, None),
        ),
        out_specs=(
            P("dp", "section", None, None),
            P("dp", "section", None, None),
            P("dp", "section", None, None),
            P("section", "dp", None),
        ),
        check_vma=False,
    )
```

```python
import functools

import jax
import jax.numpy as jnp
from jax import lax
from jax.experimental import pallas as pl
from jax.experimental.pallas import tpu as pltpu
from jax.sharding import PartitionSpec as P

PAIR = 128
CHUNKS = (2, 3)
ROWS, TWICE, SLOTS = 40, 24, 48
GRADS = ROWS + TWICE
SENT = GRADS + SLOTS
STEP = 16
SCALE = 0.125
F32 = jnp.float32
BF16 = jnp.bfloat16
VMEM_LIMIT = 60 * 1024 * 1024
SMALL = 20 * 1024 * 1024

NT = (((1,), (1,)), ((), ()))
NN = (((1,), (0,)), ((), ()))


def mm(a, b, dims=NN):
    return lax.dot_general(a, b, dims, preferred_element_type=F32)


def params(grant=VMEM_LIMIT, **kw):
    return pltpu.CompilerParams(vmem_limit_bytes=grant, **kw)


def cost(flops, bytes_accessed, transcendentals=0):
    return pl.CostEstimate(
        flops=flops, bytes_accessed=bytes_accessed, transcendentals=transcendentals
    )


def passed_along(value, axis, steps):
    count = lax.axis_size(axis)
    pairs = [(source, (source + steps) % count) for source in range(count)]
    return lax.ppermute(value, axis, pairs)


def exchanged(value):
    return lax.all_to_all(value, "dp", split_axis=0, concat_axis=0, tiled=True)


def down_the_rows(dr):
    filler = jnp.zeros((8 - dr.shape[0], dr.shape[1]), F32)
    return jnp.concatenate([dr.astype(F32), filler], axis=0).T.astype(jnp.int32)


def slots_along_lanes(dr, capacity):
    dc = down_the_rows(dr)
    rows = dr.shape[1]
    shape = (rows, rows)
    before = lax.broadcasted_iota(jnp.int32, shape, 0) < lax.broadcasted_iota(
        jnp.int32, shape, 1
    )
    found = []
    for which in range(2):
        mine = dr[which : which + 1, :]
        same = jnp.logical_or(dc[:, 0:1] == mine, dc[:, 1:2] == mine)
        earlier = jnp.where(jnp.logical_and(same, before), 1.0, 0.0)
        place = jnp.sum(earlier, axis=0, keepdims=True).astype(jnp.int32)
        found.append(mine * capacity + place)
    return found


def slots_along_sublanes(dr, capacity):
    dc = down_the_rows(dr)
    rows = dr.shape[1]
    shape = (rows, rows)
    before = lax.broadcasted_iota(jnp.int32, shape, 1) < lax.broadcasted_iota(
        jnp.int32, shape, 0
    )
    found = []
    for which in range(2):
        mine = dc[:, which : which + 1]
        same = jnp.logical_or(dr[0:1, :] == mine, dr[1:2, :] == mine)
        earlier = jnp.where(jnp.logical_and(same, before), 1.0, 0.0)
        place = jnp.sum(earlier, axis=1, keepdims=True).astype(jnp.int32)
        found.append(mine * capacity + place)
    return found


def dispatch_kernel(capacity, dr_ref, own_ref, out_ref, slot_ref):
    rows = own_ref.shape[0]
    block = pl.program_id(0)

    @pl.when(block == 0)
    def _():
        for which, slot in enumerate(slots_along_lanes(dr_ref[...], capacity)):
            slot_ref[which : which + 1, :] = slot

    at = lax.broadcasted_iota(jnp.int32, (rows, rows), 0) + block * rows
    table = jnp.logical_or(at == slot_ref[0:1, :], at == slot_ref[1:2, :])
    table = jnp.where(table, 1.0, 0.0).astype(BF16)
    both = jnp.concatenate([own_ref[...], jnp.ones((rows, PAIR), BF16)], axis=1)
    out_ref[...] = mm(table, both).astype(BF16)


def dispatch(capacity, readers, dr, own):
    rows, width = own.shape
    slots = readers * capacity
    whole = lambda i: (0, 0)
    return pl.pallas_call(
        functools.partial(dispatch_kernel, capacity),
        grid=(slots // rows,),
        in_specs=[pl.BlockSpec(dr.shape, whole), pl.BlockSpec((rows, width), whole)],
        out_specs=pl.BlockSpec((rows, width + PAIR), lambda i: (i, 0)),
        out_shape=jax.ShapeDtypeStruct((slots, width + PAIR), BF16),
        scratch_shapes=[pltpu.VMEM((8, rows), jnp.int32)],
        compiler_params=params(dimension_semantics=("arbitrary",)),
        cost_estimate=cost(2 * rows * width * slots, 2 * width * (rows + slots)),
        name="dispatch",
    )(dr, own)


def attend_kernel(held, *refs):
    q_ref, g_ref, own_ref, got_ref, wk_ref, wv_ref, entering_ref = refs[:7]
    o_ref, dq_ref, down_ref, sent_ref = refs[7 + held : 11 + held]
    kv_ref, s_ref, dp_ref, mem_t_ref, entering_t_ref = refs[11 + held :]
    readers = sent_ref.shape[0]
    dec = q_ref.shape[0]
    tile, width = own_ref.shape
    tiles = 1 + got_ref.shape[0] // tile
    lane = lax.broadcasted_iota(jnp.int32, (dec, PAIR), 1)
    q = q_ref[...] * jnp.asarray(SCALE, BF16)
    g = g_ref[...]
    zero = jnp.zeros_like(q)
    head = [lane < PAIR // 2, lane >= PAIR // 2]
    q_both = jnp.concatenate([jnp.where(head[h], q, zero) for h in range(2)], axis=0)
    g_both = jnp.concatenate([jnp.where(head[h], g, zero) for h in range(2)], axis=0)
    weights = jnp.concatenate([wk_ref[...], wv_ref[...]], axis=1)

    def frames(t):
        if t == 0:
            return own_ref[...]
        return got_ref[pl.ds((t - 1) * tile, tile), :width]

    @pl.when(pl.program_id(0) == 0)
    def _():
        for t in range(tiles):
            mem_t_ref[:, t * tile : (t + 1) * tile] = frames(t).T
        entering_t_ref[...] = entering_ref[...].T

    for t in range(tiles):
        kv_ref[pl.ds(t * tile, tile), :] = mm(frames(t), weights).astype(BF16)

    tops = []
    for t in range(tiles):
        at = pl.ds(t * tile, tile)
        s = mm(kv_ref[at, :PAIR], q_both, NT)
        if t > 0:
            flag = got_ref[pl.ds((t - 1) * tile, tile), width : width + PAIR]
            s = s + (flag.astype(F32)[:, 0:1] - 1.0) * 1e30
        s_ref[at, :] = s
        tops.append(jnp.max(s, axis=0, keepdims=True))
    top = functools.reduce(jnp.maximum, tops)
    total = jnp.zeros_like(top)
    inner = jnp.zeros_like(top)
    for t in range(tiles):
        at = pl.ds(t * tile, tile)
        e = jnp.exp(s_ref[at, :] - top)
        s_ref[at, :] = e
        total = total + jnp.sum(e, axis=0, keepdims=True)
        dp = mm(kv_ref[at, PAIR:], g_both, NT)
        dp_ref[at, :] = dp
        inner = inner + jnp.sum(e * dp, axis=0, keepdims=True)
    inverse = 1.0 / total
    inner = inner * inverse
    half = PAIR // 2
    out_t = [jnp.zeros((half, dec), F32) for _ in range(2)]
    dq_t = [jnp.zeros((half, dec), F32) for _ in range(2)]
    for t in range(tiles):
        at = pl.ds(t * tile, tile)
        kv_t = kv_ref[at, :].T
        p = s_ref[at, :] * inverse
        pb = p.astype(BF16)
        ds = (p * (dp_ref[at, :] - inner)).astype(BF16)
        for h in range(2):
            cols = slice(h * dec, (h + 1) * dec)
            dq_t[h] = dq_t[h] + mm(kv_t[h * half : (h + 1) * half], ds[:, cols])
            out_t[h] = out_t[h] + mm(kv_t[PAIR + h * half : PAIR + (h + 1) * half], pb[:, cols])
        dk = mm(ds, q_both)
        dv = mm(pb, g_both)
        dkv = jnp.concatenate([dk, dv], axis=1).astype(BF16)
        kv_ref[at, :] = dkv
        if t == 0:
            down_ref[...] = dkv
        else:
            count = tile // SLOTS
            dkv = dkv.reshape(count, SLOTS, 2 * PAIR)
            sent_ref[pl.ds((t - 1) * count, count), GRADS:, :] = dkv
    o_ref[...] = jnp.concatenate(out_t, axis=0).T.astype(BF16)
    dq = (jnp.concatenate(dq_t, axis=0) * SCALE).T.astype(BF16)
    dq_ref[...] = dq
    grad = mm(mem_t_ref[...], kv_ref[...]).reshape(readers, ROWS, 2 * PAIR)
    sent_ref[:, :ROWS, :] = grad.astype(BF16)
    grad = mm(entering_t_ref[...], dq).reshape(readers, ROWS, PAIR)
    grad = jnp.concatenate([grad[:, :TWICE], grad[:, ROWS - TWICE :]], axis=2)
    sent_ref[:, ROWS:GRADS, :] = grad.astype(BF16)


def attend(first, pairs, readers, queries, cot, own, got, wk, wv, entering, filled):
    dec, heads = queries.shape
    rows, width = own.shape
    slots = got.shape[0]
    total = rows + slots
    pair_at = lambda p: (0, first + p)
    whole = lambda p: (0, 0)
    return pl.pallas_call(
        functools.partial(attend_kernel, len(filled)),
        grid=(pairs,),
        in_specs=[
            pl.BlockSpec((dec, PAIR), pair_at),
            pl.BlockSpec((dec, PAIR), pair_at),
            pl.BlockSpec((rows, width), whole),
            pl.BlockSpec((slots, width + PAIR), whole),
            pl.BlockSpec((width, PAIR), pair_at),
            pl.BlockSpec((width, PAIR), pair_at),
            pl.BlockSpec((dec, width), whole),
        ]
        + [pl.BlockSpec(memory_space=pl.ANY)] * len(filled),
        out_specs=[
            pl.BlockSpec((dec, PAIR), pair_at),
            pl.BlockSpec((dec, PAIR), pair_at),
            pl.BlockSpec((rows, 2 * PAIR), pair_at),
            pl.BlockSpec((readers, SENT, 2 * PAIR), lambda p: (0, 0, p)),
        ],
        out_shape=(
            jax.ShapeDtypeStruct((dec, heads), BF16),
            jax.ShapeDtypeStruct((dec, heads), BF16),
            jax.ShapeDtypeStruct((rows, 2 * heads), BF16),
            jax.ShapeDtypeStruct((readers, SENT, 2 * PAIR * pairs), BF16),
        ),
        scratch_shapes=[
            pltpu.VMEM((total, 2 * PAIR), BF16),
            pltpu.VMEM((total, 2 * dec), F32),
            pltpu.VMEM((total, 2 * dec), F32),
            pltpu.VMEM((width, total), BF16),
            pltpu.VMEM((width, dec), BF16),
        ],
        input_output_aliases={7 + i: i for i in range(len(filled))},
        compiler_params=params(dimension_semantics=("arbitrary",)),
        cost_estimate=cost(
            pairs * (12 * dec * total * PAIR * 4 + 8 * width * total * PAIR),
            2 * total * width + pairs * 12 * total * PAIR,
            pairs * 2 * dec * total,
        ),
        name=f"attend_{first}",
    )(queries, cot, own, got, wk, wv, entering, *filled)


def query_kernel(dq_ref, wq_ref, dent_ref):
    dent_ref[...] = mm(dq_ref[...], wq_ref[...], NT).astype(BF16)


def query_side(dq, wq):
    dec = dq.shape[0]
    width, heads = wq.shape
    return pl.pallas_call(
        query_kernel,
        out_shape=jax.ShapeDtypeStruct((dec, width), BF16),
        compiler_params=params(SMALL),
        cost_estimate=cost(2 * dec * width * heads, 2 * width * (dec + heads)),
        name="query_side",
    )(dq, wq)


def table_kernel(capacity, dr_ref, out_ref):
    rows = out_ref.shape[0]
    slot_a, slot_b = slots_along_sublanes(dr_ref[...], capacity)
    for block in range(out_ref.shape[1] // rows):
        at = lax.broadcasted_iota(jnp.int32, (rows, rows), 1) + block * rows
        table = jnp.logical_or(at == slot_a, at == slot_b)
        out_ref[:, block * rows : (block + 1) * rows] = jnp.where(table, 1.0, 0.0).astype(BF16)


def table_of(capacity, readers, dr):
    shape = (dr.shape[1], readers * capacity)
    return pl.pallas_call(
        functools.partial(table_kernel, capacity),
        out_shape=jax.ShapeDtypeStruct(shape, BF16),
        compiler_params=params(SMALL),
        cost_estimate=cost(0, 2 * shape[0] * shape[1]),
        name="table_of",
    )(dr)


def combine_kernel(held, table_ref, down_ref, wk_ref, wv_ref, *refs):
    views = refs[: SLOTS // STEP]
    out_ref, sum_ref = refs[-2:]
    lanes = down_ref.shape[1]
    p = pl.program_id(0)
    back = jnp.concatenate([v[...] for v in views], axis=1).reshape(-1, lanes)
    tot = (down_ref[...].astype(F32) + mm(table_ref[...], back)).astype(BF16)
    weights = jnp.concatenate([wk_ref[...], wv_ref[...]], axis=1)
    out = mm(tot, weights, NT)

    @pl.when(p == 0)
    def _():
        sum_ref[...] = out + refs[SLOTS // STEP][...] if held else out

    @pl.when(p > 0)
    def _():
        sum_ref[...] += out

    @pl.when(p == pl.num_programs(0) - 1)
    def _():
        out_ref[...] = sum_ref[...].astype(out_ref.dtype)


def combine(first, last, table, down, back, wk, wv, held):
    rows = down.shape[0]
    width = wk.shape[0]
    readers, _, lanes = back.shape
    pairs = lanes // (2 * PAIR)
    whole = lambda p: (0, 0)
    pair_at = lambda p: (0, first + p)
    full = lambda a: pl.BlockSpec(a.shape, whole)
    view = lambda i: pl.BlockSpec((readers, STEP, 2 * PAIR), lambda p: (0, GRADS // STEP + i, p))
    return pl.pallas_call(
        functools.partial(combine_kernel, len(held)),
        grid=(pairs,),
        in_specs=[
            full(table),
            pl.BlockSpec((rows, 2 * PAIR), pair_at),
            pl.BlockSpec((width, PAIR), pair_at),
            pl.BlockSpec((width, PAIR), pair_at),
        ]
        + [view(i) for i in range(SLOTS // STEP)]
        + [full(h) for h in held],
        out_specs=pl.BlockSpec((rows, width), whole),
        out_shape=jax.ShapeDtypeStruct((rows, width), BF16 if last else F32),
        scratch_shapes=[pltpu.VMEM((rows, width), F32)],
        compiler_params=params(SMALL, dimension_semantics=("arbitrary",)),
        cost_estimate=cost(
            2 * rows * lanes * (width + readers * SLOTS),
            2 * (rows * width + width * lanes + readers * SLOTS * lanes),
        ),
        name=f"combine_{first}",
    )(table, down, wk, wv, *([back] * (SLOTS // STEP)), *held)


def sum_kernel(first, last, back_ref, *refs):
    held, out_ref = refs[:-1], refs[-1]

    def added(lanes):
        sums = [back_ref[a, :, lanes].astype(F32) for a in range(4)]
        for a in range(4, back_ref.shape[0]):
            sums[a % 4] = sums[a % 4] + back_ref[a, :, lanes].astype(F32)
        return (sums[0] + sums[1]) + (sums[2] + sums[3])

    upper, lower = added(slice(0, PAIR)), added(slice(PAIR, 2 * PAIR))
    if not last:
        out_ref[...] = jnp.concatenate([upper, lower], axis=1)
        return
    heads = out_ref.shape[1] // 3

    def place(pair, upper, lower):
        at = [pl.ds(pl.multiple_of(part * heads + pair * PAIR, PAIR), PAIR) for part in range(3)]
        out_ref[:TWICE, at[0]] = upper[ROWS:]
        out_ref[TWICE:, at[0]] = lower[2 * TWICE :]
        out_ref[:, at[1]] = upper[:ROWS]
        out_ref[:, at[2]] = lower[:ROWS]

    place(first + pl.program_id(0), upper, lower)

    @pl.when(pl.program_id(0) == 0)
    def _():
        pair = 0
        for r in held:
            for c in range(0, r.shape[1], 2 * PAIR):
                place(pair, r[:, c : c + PAIR], r[:, c + PAIR : c + 2 * PAIR])
                pair += 1


def summed(first, last, heads, back, held):
    readers, _, lanes = back.shape
    shape = (ROWS, 3 * heads) if last else (GRADS, lanes)
    whole = lambda p: (0, 0)
    here = pl.BlockSpec((GRADS, 2 * PAIR), lambda p: (0, p))
    return pl.pallas_call(
        functools.partial(sum_kernel, first, last),
        grid=(lanes // (2 * PAIR),),
        in_specs=[pl.BlockSpec((readers, GRADS, 2 * PAIR), lambda p: (0, 0, p))]
        + [pl.BlockSpec(h.shape, whole) for h in held],
        out_specs=pl.BlockSpec(shape, whole) if last else here,
        out_shape=jax.ShapeDtypeStruct(shape, F32),
        compiler_params=params(SMALL, dimension_semantics=("arbitrary",)),
        cost_estimate=cost(readers * GRADS * lanes, 2 * readers * GRADS * lanes),
        name=f"summed_{first}",
    )(back, *held)


def per_device(encoder, destinations, hidden, w_query, w_key, w_value, cotangent):
    own = encoder[0, 0]
    dest = destinations[0, 0]
    wq, wk, wv = w_query[0], w_key[0], w_value[0]
    cot = cotangent[0, 0]
    rows, width = own.shape
    heads = wq.shape[1]
    readers = lax.axis_size("dp")
    capacity = 4 * rows // readers

    slots = readers * capacity

    slots = readers * capacity

    entering = passed_along(hidden[0, 0], "section", 1)
    out = dispatch(capacity, readers, dest.T, own)
    out, entering = lax.optimization_barrier((out, entering))
    queries = jnp.dot(entering, wq, preferred_element_type=F32).astype(BF16)
    got = exchanged(out.reshape(readers, capacity, -1)).reshape(slots, -1)

    filled, backs, firsts, first = (), [], [], 0
    for pairs in CHUNKS:
        *filled, sent = attend(
            first, pairs, readers, queries, cot, own, got, wk, wv, entering, filled
        )
        firsts.append(first)
        first += pairs
        backs.append(exchanged(sent))
    attended, dq, down = filled
    dentering = query_side(dq, wq)
    table = table_of(capacity, readers, dest.T)

    held, grads = [], []
    for c, first in enumerate(firsts):
        last = c == len(firsts) - 1
        if held:
            backs[c], held, grads, down, dentering, table = lax.optimization_barrier(
                (backs[c], held, grads, down, dentering, table)
            )
        if last:
            d_hidden = passed_along(dentering, "section", -1)
        held = [combine(first, last, table, down, backs[c], wk, wv, held)]
        grads.append(summed(first, last, heads, backs[c], grads))
    d_enc = held[0]
    grads = grads[-1]
    return (attended[None, None], d_hidden[None, None], d_enc[None, None], grads[None])


def solution(mesh):
    return jax.shard_map(
        per_device,
        mesh=mesh,
        in_specs=(
            P("dp", "section", None, None),
            P("dp", "section", None, None),
            P("dp", "section", None, None),
            P("section", None, None),
            P("section", None, None),
            P("section", None, None),
            P("dp", "section", None, None),
        ),
        out_specs=(
            P("dp", "section", None, None),
            P("dp", "section", None, None),
            P("dp", "section", None, None),
            P("section", "dp", None),
        ),
        check_vma=False,
    )
```
